128 devices in a mesh: rows: 8 (over z, core), cache: 16 (over x, y).
Axes of the slice: x: 4, y: 4, z: 4, core: 2. Of those that a mesh axis runs over, the one named last changes fastest.
Arguments:
- queries: bfloat16 [32, 128, 576], P('rows', 'cache'), may hold values from -20 to 20
- prefix_cache: bfloat16 [256, 1024, 576], P(('rows', 'cache')), may hold values from -12 to 12
- suffix_cache: bfloat16 [32, 1024, 576], P('rows'), may hold values from -12 to 12
- suffix_len: int32 [32], P('rows'), may hold values from 2 to 1024, as said below
- touch_mask: int32 [32, 256], replicated, may hold values from 0 to 1, as said below
- block_slot: int32 [256], replicated, may hold values from 0 to 255, as said below
Outputs:
- latent_out: bfloat16 [32, 128, 512], P('rows', 'cache')
- lse_out: float32 [32, 128], P('rows', 'cache')
The draws below stay inside these ranges and needn't reach their ends.
Inputs may be any that keep to these rules, and one draw needn't show every extreme that they name: `suffix_len`: some request has exactly 1024 suffix tokens. `touch_mask`: each request touches 4 to 16 logical blocks; some request touches exactly 4 and some exactly 16. Within each aligned block of 4 requests, at most 2 requests read blocks held by any one holder, and in every such block some holder is read by exactly 2 of them. `block_slot`: each slot holds exactly one logical block.
All inputs are finite; a program needn't handle non-finite values.
Results may differ from the reference program's by a relative error of at most 0.0048.
Values may be sent and summed in bfloat16 or wider, within the bound.
No kernel may reach another device: no remote copies, remote signals or barrier semaphores. Data moves between devices by JAX's collectives and lax.ppermute only.
A program may use at most 64 MiB of HBM per device.

```python
import math
import jax
import jax.numpy as jnp
from jax import lax

H = 128
LAT = 512
DK = 576
BLK = 1024
BLK_DEV = 2
SUF = 1024
TOUCH_MIN = 4
TOUCH_MAX = 16
REQ_DEV = 4
SHARE = 2
REQ = 32
NBLK = 256


def token_scales(key, shape):
    return jnp.exp(jax.random.uniform(key, shape, jnp.float32, math.log(0.3), math.log(3.0)))


def draw_queries(key, part):
    key = jax.random.fold_in(key, 11)
    base_key = jax.random.fold_in(key, 0)
    entries = jnp.clip(jax.random.normal(base_key, (REQ, H, DK), jnp.float32), -6.0, 6.0)
    return entries.astype(jnp.bfloat16)


def draw_prefix_cache(key, part):
    key = jax.random.fold_in(key, 12)
    base_key, scale_key = jax.random.split(key, 2)
    scales = token_scales(scale_key, (NBLK, BLK, 1))
    entries = jnp.clip(jax.random.normal(base_key, (NBLK, BLK, DK), jnp.float32), -4.0, 4.0) * scales
    return entries.astype(jnp.bfloat16)


def draw_suffix_cache(key, part):
    key = jax.random.fold_in(key, 13)
    base_key, scale_key = jax.random.split(key, 2)
    scales = token_scales(scale_key, (REQ, SUF, 1))
    entries = jnp.clip(jax.random.normal(base_key, (REQ, SUF, DK), jnp.float32), -4.0, 4.0) * scales
    return entries.astype(jnp.bfloat16)


def draw_suffix_len(key, part):
    key = jax.random.fold_in(key, 22)
    lengths = jax.random.randint(key, (REQ,), 2, SUF + 1)
    return lengths.at[0].set(SUF).astype(jnp.int32)


def lax_top(scored):
    return jax.lax.top_k(scored, TOUCH_MAX)[0]


def block_layout(key):
    key = jax.random.fold_in(key, 31)
    slot_key, count_key, rank_key, noise_key = jax.random.split(key, 4)
    block_slot = jax.random.permutation(slot_key, NBLK).astype(jnp.int32)
    classes = REQ_DEV // SHARE
    requests = jnp.arange(REQ, dtype=jnp.int32)
    blocks = jnp.arange(NBLK, dtype=jnp.int32)
    group = requests // REQ_DEV
    request_class = requests % REQ_DEV // SHARE
    holder_of = block_slot // BLK_DEV
    allowed = (holder_of[None, :] + group[:, None]) % classes == request_class[:, None]
    inverse = jnp.argsort(block_slot).astype(jnp.int32)
    chosen_holder = (request_class - group) % classes
    designated = inverse[chosen_holder * BLK_DEV]
    counts = jax.random.randint(count_key, (REQ,), TOUCH_MIN, TOUCH_MAX + 1)
    counts = counts.at[0].set(TOUCH_MAX).at[1].set(TOUCH_MIN)
    popularity = jax.random.permutation(rank_key, NBLK)
    weight = jnp.where(popularity < max(NBLK // 16, 1), 11, 10).astype(jnp.int32)
    noise = jax.random.randint(noise_key, (REQ, NBLK), 0, 65536)
    scored = noise * weight[None, :] * NBLK + blocks[None, :]
    is_designated = blocks[None, :] == designated[:, None]
    scored = jnp.where(is_designated, 65536 * 12 * NBLK, scored)
    scored = jnp.where(allowed | is_designated, scored, -1)
    leaders = lax_top(scored)
    threshold = jnp.take_along_axis(leaders, (counts - 1)[:, None], axis=1)
    touch_mask = (scored >= threshold).astype(jnp.int32)
    return (block_slot, touch_mask)


def draw_block_slot(key, part):
    return block_layout(key)[0]


def draw_touch_mask(key, part):
    return block_layout(key)[1]


def setup_inputs(seed: int = 0) -> dict:
    streams_of = jax.random.split(jax.random.key(seed), 7)
    return {
        "queries": draw_queries(jax.random.fold_in(streams_of[6], 71), 0),
        "prefix_cache": draw_prefix_cache(jax.random.fold_in(streams_of[6], 71), 0),
        "suffix_cache": draw_suffix_cache(jax.random.fold_in(streams_of[6], 71), 0),
        "suffix_len": draw_suffix_len(jax.random.fold_in(streams_of[6], 71), 0),
        "touch_mask": draw_touch_mask(jax.random.fold_in(streams_of[6], 71), 0),
        "block_slot": draw_block_slot(jax.random.fold_in(streams_of[6], 71), 0),
    }


SOFTMAX_SCALE = 192.0 ** -0.5
MASKED_SCORE = -1.0e30


def attend(query_rows, key_rows, live_keys):
    scores = jnp.dot(query_rows, key_rows.T, preferred_element_type=jnp.float32) * SOFTMAX_SCALE
    scores = jnp.where(live_keys[None, :], scores, MASKED_SCORE)
    row_max = jnp.max(scores, axis=1)
    exponent = jnp.exp(scores - row_max[:, None])
    totals = jnp.sum(exponent, axis=1)
    weights = exponent.astype(jnp.bfloat16)
    partial_value = jnp.dot(weights, key_rows[:, :LAT], preferred_element_type=jnp.float32) / totals[:, None]
    return partial_value, row_max + jnp.log(totals)


def combine(parts_out, parts_lse, suffix_out, suffix_lse):
    ceiling = jnp.maximum(jnp.max(parts_lse, axis=0), suffix_lse)
    part_weight = jnp.exp(parts_lse - ceiling[None])
    suffix_weight = jnp.exp(suffix_lse - ceiling)
    merged_total = suffix_weight + jnp.sum(part_weight, axis=0)
    merged = suffix_weight[..., None] * suffix_out + jnp.sum(part_weight[..., None] * parts_out.astype(jnp.float32), axis=0)
    return (merged / merged_total[..., None]).astype(jnp.bfloat16), ceiling + jnp.log(merged_total)


def reference(queries, prefix_cache, suffix_cache, suffix_len, touch_mask, block_slot):
    holders = NBLK // BLK_DEV
    matches = block_slot[:, None] == jnp.arange(NBLK, dtype=jnp.int32)[None, :]
    slot_touch = jnp.dot(touch_mask.astype(jnp.float32), matches.astype(jnp.float32)) > 0.5
    slot_touch = slot_touch.reshape(REQ, holders, BLK_DEV)

    def per_request(request):
        query_rows = queries[request]

        def per_holder(holder):
            touched = slot_touch[request, holder]

            def compute(unused):
                key_rows = lax.dynamic_slice_in_dim(prefix_cache, holder * BLK_DEV, BLK_DEV, 0).reshape(BLK_DEV * BLK, DK)
                partial_value, log_total = attend(query_rows, key_rows, jnp.repeat(touched, BLK))
                return partial_value.astype(jnp.bfloat16), log_total

            def vacant(unused):
                return jnp.zeros((H, LAT), jnp.bfloat16), jnp.full((H,), MASKED_SCORE, jnp.float32)

            return lax.cond(jnp.any(touched), compute, vacant, 0)

        holder_out, holder_lse = lax.map(per_holder, jnp.arange(holders, dtype=jnp.int32))
        positions = jnp.arange(SUF, dtype=jnp.int32)
        suffix_out, suffix_lse = attend(query_rows, suffix_cache[request], positions < suffix_len[request])
        return combine(holder_out, holder_lse, suffix_out, suffix_lse)

    latent_out, lse_out = lax.map(per_request, jnp.arange(REQ, dtype=jnp.int32))
    return latent_out, lse_out
```

```python
import functools
import jax
import jax.numpy as jnp
from jax import lax
from jax.experimental import pallas as pl
from jax.experimental.pallas import tpu as pltpu
from jax.sharding import Mesh, PartitionSpec as P

H = 128
LAT = 512
DK = 576
BLK = 1024
BLK_DEV = 2
SUF = 1024
DEVS = 128
ROWS = 8
PACK = 640
GROUPS = 8
GROUP_ROWS = 128

SOFTMAX_SCALE = 192.0 ** (-0.5)
MASKED_SCORE = -1e30
BF = jnp.bfloat16
F32 = jnp.float32
MIB = 1024 * 1024


def iota(shape, dim):
    return lax.broadcasted_iota(jnp.int32, shape, dim)


def ones_where(mask):
    return jnp.where(mask, 1.0, 0.0).astype(BF)


def dot(a, b, ca=1, cb=0):
    return lax.dot_general(a, b, (((ca,), (cb,)), ((), ())), preferred_element_type=F32)


def route_kernel(offset, me_ref, q_ref, touch_ref, slot_ref, send_ref, route_ref, table_ref):
    me = me_ref[0]
    group = lax.shift_right_logical(me, 4)
    n = DEVS * ROWS
    blocks = touch_ref.shape[1]
    onehot = ones_where(iota((blocks, blocks), 0) == slot_ref[...])
    touched = dot(onehot, touch_ref[...].astype(F32).astype(BF), 1, 1)
    touched = touched.astype(BF)
    reqs = touched.shape[1]
    mine = ones_where(iota((reqs, 32), 0) == group * 4 + lax.shift_right_logical(iota((reqs, 32), 1), 3))
    mine_touched = dot(touched, mine).astype(BF)
    row = iota((n, blocks), 0)
    holder = lax.shift_right_logical(iota((n, blocks), 1), 1)
    dev = lax.shift_right_logical(row, 3)
    same_chip = (lax.shift_right_logical(holder, 5) == lax.shift_right_logical(dev, 5)) & (
        (holder & 15) == (dev & 15)
    )
    chip_touch = jnp.minimum(dot(ones_where(same_chip), mine_touched), 1.0)
    earlier = lax.shift_right_logical(iota((32, 32), 0), 3) < lax.shift_right_logical(iota((32, 32), 1), 3)
    earlier = ones_where(earlier & ((iota((32, 32), 0) & 7) == 0))
    rank = dot(chip_touch.astype(BF), earlier)
    row = iota((n, 32), 0)
    slot = (lax.shift_right_logical(row, 2) & 1) + offset
    head = (lax.shift_right_logical(row, 7) & 1) * 4 + (row & 3)
    chosen = (chip_touch > 0.5) & (rank == slot.astype(F32)) & ((iota((n, 32), 1) & 7) == head)
    chosen = ones_where(chosen)
    route_ref[...] = chosen
    send_ref[...] = dot(chosen, q_ref[...]).astype(BF)
    b = iota((8, blocks), 0)
    owner = jnp.where(b < 2, me, me ^ 16)
    wanted = jnp.where(b < 4, owner * 2 + (b & 1), -1)
    block_touch = dot(ones_where(iota((8, blocks), 1) == wanted), touched)
    any_touch = jnp.max(block_touch, axis=0, keepdims=True)
    any_touch = jnp.broadcast_to(any_touch, (8, reqs))
    before = (lax.shift_right_logical(iota((reqs, reqs), 0), 2) == lax.shift_right_logical(iota((reqs, reqs), 1), 2)) & (
        iota((reqs, reqs), 0) < iota((reqs, reqs), 1)
    )
    place = dot(any_touch.astype(BF), ones_where(before))
    in_group = ones_where(lax.shift_right_logical(iota((reqs, 128), 0), 2) == iota((reqs, 128), 1))
    first = dot(jnp.where(place == float(offset), block_touch, 0.0).astype(BF), in_group)
    second = dot(jnp.where(place == float(offset + 1), block_touch, 0.0).astype(BF), in_group)
    chip = iota((64, blocks), 0)
    holder = lax.shift_right_logical(iota((64, blocks), 1), 1)
    of_chip = (lax.shift_right_logical(holder, 5) == lax.shift_right_logical(chip, 4)) & (
        (holder & 15) == (chip & 15)
    )
    on_chip = jnp.minimum(dot(ones_where(of_chip), touched), 1.0).astype(BF)
    most = jnp.max(jnp.max(dot(on_chip, in_group), axis=0, keepdims=True), axis=1, keepdims=True)
    bits = (first + 2.0 * second).astype(jnp.int32)
    table_ref[...] = jnp.where(iota((8, 128), 0) == 7, most.astype(jnp.int32), bits)


def route(offset, me, q_rows, touch_mask, block_slot):
    n = DEVS * ROWS
    vmem = pl.BlockSpec(memory_space=pltpu.VMEM)
    return pl.pallas_call(
        functools.partial(route_kernel, offset),
        out_shape=(
            jax.ShapeDtypeStruct((n, DK), BF),
            jax.ShapeDtypeStruct((n, 32), BF),
            jax.ShapeDtypeStruct((8, 128), jnp.int32),
        ),
        in_specs=[pl.BlockSpec(memory_space=pltpu.SMEM), vmem, vmem, vmem],
        out_specs=(vmem, vmem, vmem),
        compiler_params=pltpu.CompilerParams(vmem_limit_bytes=32 * MIB),
        cost_estimate=pl.CostEstimate(flops=2 * n * 32 * 1024, bytes_accessed=2 * n * DK, transcendentals=0),
        name="route",
    )(me, q_rows, touch_mask, block_slot.reshape(1, -1))


def holder_kernel(table_ref, q_ref, own_ref, peer_ref, out_ref, keys, top, total, acc, sems):
    copies = []
    for b in range(4):
        src = own_ref if b < 2 else peer_ref
        copies.append(pltpu.make_async_copy(src.at[b & 1], keys.at[b], sems.at[b]))
        copies[-1].start()
    top[...] = jnp.full(top.shape, MASKED_SCORE, F32)
    total[...] = jnp.ones(total.shape, F32)
    acc[...] = jnp.zeros(acc.shape, F32)
    for b in range(4):
        copies[b].wait()

        def step(g, carry, b=b):
            bits = table_ref[b, g]

            @pl.when(bits > 0)
            def _():
                s = dot(q_ref[g], keys[b], 1, 1) * SOFTMAX_SCALE
                second = (lax.shift_right_logical(iota((GROUP_ROWS, 1), 0), 2) & 1) == 1
                live = jnp.where(second, lax.shift_right_logical(bits, 1), bits & 1) > 0
                s = jnp.where(live, s, MASKED_SCORE)
                old = top[g]
                new = jnp.maximum(old, jnp.max(s, axis=1, keepdims=True))
                scale = jnp.exp(old - new)
                p = jnp.exp(s - new)
                top[g] = new
                total[g] = total[g] * scale + jnp.sum(p, axis=1, keepdims=True)
                acc[g] = acc[g] * scale + dot(p.astype(BF), keys[b, :, :LAT])

            return carry

        lax.fori_loop(0, GROUPS, step, 0)

    def finish(g, carry):
        out_ref[g, :, :LAT] = (acc[g] / total[g]).astype(BF)
        lse = top[g] + jnp.log(total[g])
        high = lse.astype(BF).astype(F32)
        middle = (lse - high).astype(BF).astype(F32)
        low = lse - high - middle
        lane = iota((GROUP_ROWS, PACK - LAT), 1)
        tail = jnp.where(lane == 0, high, 0.0)
        tail = jnp.where(lane == 1, middle, tail)
        tail = jnp.where(lane == 2, low, tail)
        tail = jnp.where(lane == 3, 1.0, tail)
        out_ref[g, :, LAT:] = tail.astype(BF)
        return carry

    lax.fori_loop(0, GROUPS, finish, 0)


def holder(table, queries, own, peer):
    return pl.pallas_call(
        holder_kernel,
        out_shape=jax.ShapeDtypeStruct((GROUPS, GROUP_ROWS, PACK), BF),
        in_specs=[
            pl.BlockSpec(memory_space=pltpu.SMEM),
            pl.BlockSpec(memory_space=pltpu.VMEM),
            pl.BlockSpec(memory_space=pl.ANY),
            pl.BlockSpec(memory_space=pl.ANY),
        ],
        out_specs=pl.BlockSpec(memory_space=pltpu.VMEM),
        scratch_shapes=[
            pltpu.VMEM((4, BLK, DK), BF),
            pltpu.VMEM((GROUPS, GROUP_ROWS, 1), F32),
            pltpu.VMEM((GROUPS, GROUP_ROWS, 1), F32),
            pltpu.VMEM((GROUPS, GROUP_ROWS, LAT), F32),
            pltpu.SemaphoreType.DMA((4,)),
        ],
        compiler_params=pltpu.CompilerParams(vmem_limit_bytes=40 * MIB),
        cost_estimate=pl.CostEstimate(
            flops=2 * 1024 * 1024 * (DK + LAT), bytes_accessed=4 * 2 * BLK * DK, transcendentals=1024 * 1024
        ),
        name="holder",
    )(table, queries, own, peer)


def suffix_kernel(len_ref, q_ref, kv_ref, out_ref, lse_ref):
    r = pl.program_id(0)
    kv = kv_ref[0]
    s = dot(q_ref[0], kv, 1, 1) * SOFTMAX_SCALE
    s = jnp.where(iota(s.shape, 1) < len_ref[r], s, MASKED_SCORE)
    top = jnp.max(s, axis=1, keepdims=True)
    p = jnp.exp(s - top)
    total = jnp.sum(p, axis=1, keepdims=True)
    out_ref[0] = dot(p.astype(BF), kv[:, :LAT]) / total
    lse_ref[0] = jnp.broadcast_to(top + jnp.log(total), lse_ref.shape[1:])


def suffix(lengths, queries, cache):
    reqs, heads, _ = queries.shape
    return pl.pallas_call(
        suffix_kernel,
        grid=(reqs,),
        out_shape=(
            jax.ShapeDtypeStruct((reqs, heads, LAT), F32),
            jax.ShapeDtypeStruct((reqs, heads, 128), F32),
        ),
        in_specs=[
            pl.BlockSpec(memory_space=pltpu.SMEM),
            pl.BlockSpec((1, heads, DK), lambda r: (r, 0, 0)),
            pl.BlockSpec((1, SUF, DK), lambda r: (r, 0, 0)),
        ],
        out_specs=(
            pl.BlockSpec((1, heads, LAT), lambda r: (r, 0, 0)),
            pl.BlockSpec((1, heads, 128), lambda r: (r, 0, 0)),
        ),
        compiler_params=pltpu.CompilerParams(vmem_limit_bytes=32 * MIB),
        cost_estimate=pl.CostEstimate(
            flops=2 * 4 * 256 * 1024 * (DK + LAT), bytes_accessed=4 * 2 * SUF * DK, transcendentals=4 * 8 * 1024
        ),
        name="suffix",
    )(lengths, queries, cache)


def merge_kernel(rounds, *refs):
    parts, routes = refs[:rounds], refs[rounds : 2 * rounds]
    suffix_ref, suffix_lse_ref, out_ref, lse_ref = refs[2 * rounds :]
    heads = 32
    eye = iota((heads, heads), 0) == iota((heads, heads), 1)
    suffix_lse = suffix_lse_ref[:, :1]
    ceiling = jnp.max(jnp.where(eye, suffix_lse, MASKED_SCORE), axis=0, keepdims=True)
    scores = []
    for part, chosen in zip(parts, routes):
        tail = part[:, LAT:].astype(F32)
        lse = tail[:, 0:1] + tail[:, 1:2] + tail[:, 2:3]
        score = jnp.where(chosen[...] > 0.5, lse, MASKED_SCORE)
        scores.append(score)
        ceiling = jnp.maximum(ceiling, jnp.max(score, axis=0, keepdims=True))
    top = jnp.max(jnp.where(eye, ceiling, MASKED_SCORE), axis=1, keepdims=True)
    weight = jnp.exp(suffix_lse - top)
    merged = weight * suffix_ref[...]
    total = weight
    for part, score in zip(parts, scores):
        w = jnp.exp(score - ceiling)
        high = w.astype(BF)
        low = (w - high.astype(F32)).astype(BF)
        both = jnp.concatenate([high, low], axis=1).T
        sums = dot(both, part[...])
        sums = sums[:heads] + sums[heads:]
        merged = merged + sums[:, :LAT]
        total = total + sums[:, LAT + 3 : LAT + 4]
    out_ref[...] = (merged / total).astype(BF)
    lse_ref[...] = jnp.broadcast_to(top + jnp.log(total), lse_ref.shape)


def merge(parts, routes, suffix_out, suffix_lse):
    vmem = pl.BlockSpec(memory_space=pltpu.VMEM)
    out, lse = pl.pallas_call(
        functools.partial(merge_kernel, len(parts)),
        out_shape=(jax.ShapeDtypeStruct((32, LAT), BF), jax.ShapeDtypeStruct((32, 128), F32)),
        in_specs=[vmem] * (2 * len(parts) + 2),
        out_specs=(vmem, vmem),
        compiler_params=pltpu.CompilerParams(vmem_limit_bytes=32 * MIB),
        name="merge",
    )(*parts, *routes, suffix_out, suffix_lse)
    return out, lse[:, 0]


AXES = ("z", "core", "x", "y")


def on_device(queries, prefix_cache, suffix_cache, suffix_len, touch_mask, block_slot):
    reqs, heads, _ = queries.shape
    me = lax.axis_index(AXES).astype(jnp.int32).reshape(1)
    q_rows = queries.reshape(reqs * heads, DK)
    peer = lax.ppermute(prefix_cache, "core", [(0, 1), (1, 0)])

    def one_round(offset, peer):
        send, chosen, table = route(offset, me, q_rows, touch_mask, block_slot)
        got = lax.all_to_all(send.reshape(DEVS, ROWS, DK), AXES, split_axis=0, concat_axis=0, tiled=True)
        parts = holder(table, got.reshape(GROUPS, GROUP_ROWS, DK), prefix_cache, peer)
        parts = lax.all_to_all(parts.reshape(DEVS, ROWS, PACK), AXES, split_axis=0, concat_axis=0, tiled=True)
        return parts.reshape(DEVS * ROWS, PACK), chosen, table

    parts, chosen, table = one_round(0, peer)
    suffix_out, suffix_lse = suffix(suffix_len, queries, suffix_cache)
    suffix_out = suffix_out.reshape(reqs * heads, LAT)
    suffix_lse = suffix_lse.reshape(reqs * heads, 128)

    def one(parts, chosen, peer):
        return merge([parts], [chosen], suffix_out, suffix_lse)

    def two(parts, chosen, peer):
        more, more_chosen, _ = one_round(2, peer)
        return merge([parts, more], [chosen, more_chosen], suffix_out, suffix_lse)

    out, lse = lax.cond(table[7, 0] > 2, two, one, parts, chosen, peer)
    return out.reshape(reqs, heads, LAT), lse.reshape(reqs, heads)


def solution(mesh):
    grid = Mesh(mesh.devices.reshape(4, 2, 4, 4), AXES)
    rows, cache = ("z", "core"), ("x", "y")
    in_specs = (
        P(rows, cache, None),
        P(AXES, None, None),
        P(rows, None, None),
        P(rows),
        P(),
        P(),
    )
    out_specs = (P(rows, cache, None), P(rows, cache))
    return jax.shard_map(
        on_device, mesh=grid, in_specs=in_specs, out_specs=out_specs, check_vma=False
    )
```

```python
import functools
import jax
import jax.numpy as jnp
from jax import lax
from jax.experimental import pallas as pl
from jax.experimental.pallas import tpu as pltpu
from jax.sharding import Mesh, PartitionSpec as P

H = 128
LAT = 512
DK = 576
BLK = 1024
BLK_DEV = 2
SUF = 1024
DEVS = 128
ROWS = 8
PACK = 640
GROUPS = 8
GROUP_ROWS = 128

SOFTMAX_SCALE = 192.0 ** (-0.5)
MASKED_SCORE = -1e30
BF = jnp.bfloat16
F32 = jnp.float32
MIB = 1024 * 1024


def iota(shape, dim):
    return lax.broadcasted_iota(jnp.int32, shape, dim)


def ones_where(mask):
    return jnp.where(mask, 1.0, 0.0).astype(BF)


def dot(a, b, ca=1, cb=0):
    return lax.dot_general(a, b, (((ca,), (cb,)), ((), ())), preferred_element_type=F32)


def route_kernel(offset, me_ref, q_ref, touch_ref, slot_ref, send_ref, route_ref, table_ref, stage, sems):
    me = me_ref[0]
    group = lax.shift_right_logical(me, 4)
    n = DEVS * ROWS
    chips = DEVS // 2
    touch = touch_ref[...].astype(F32).astype(BF)
    reqs, blocks = touch.shape
    slots = slot_ref[...]
    chip_of = lax.shift_right_logical(slots, 6) * 16 + (lax.shift_right_logical(slots, 1) & 15)
    chip_touch = dot(ones_where(iota((chips, blocks), 0) == chip_of), touch, 1, 1)
    chip_touch = jnp.minimum(chip_touch, 1.0)
    of_group = lax.shift_right_logical(iota((reqs, reqs), 0), 2)
    before = ones_where(
        (of_group == lax.shift_right_logical(iota((reqs, reqs), 1), 2)) & (iota((reqs, reqs), 0) < iota((reqs, reqs), 1))
    )
    rank = dot(chip_touch.astype(BF), before)
    mine = ones_where(iota((reqs, 32), 0) == group * 4 + lax.shift_right_logical(iota((reqs, 32), 1), 3))
    first = ((group & 1) + offset).astype(F32)
    second = ((1 - (group & 1)) + offset).astype(F32)
    by_core = [jnp.where(rank == want, chip_touch, 0.0) for want in (first, second)]
    by_dev = [by_core[k][z * 16 : z * 16 + 16] for z in range(4) for k in (0, 1)]
    by_dev = dot(jnp.concatenate(by_dev, axis=0).astype(BF), mine)
    part = 256
    copies = []
    for i in range(n // part):
        chosen = by_dev[i * part // ROWS : (i + 1) * part // ROWS]
        chosen = jnp.broadcast_to(chosen[:, None, :], (part // ROWS, ROWS, 32)).reshape(part, 32)
        chosen = jnp.where((iota((part, 32), 1) & 7) == (iota((part, 32), 0) & 7), chosen, 0.0).astype(BF)
        here = pl.ds(i * part, part)
        route_ref[here, :] = chosen
        stage[here, :] = dot(chosen, q_ref[...]).astype(BF)
        copies.append(pltpu.make_async_copy(stage.at[here], send_ref.at[here], sems.at[i]))
        copies[-1].start()
    core = lax.shift_right_logical(me, 4) & 1
    b = iota((8, blocks), 0)
    owner = jnp.where(b < 2, me, me ^ 16)
    wanted = jnp.where(b < 4, owner * 2 + (b & 1), -1)
    block_touch = dot(ones_where(slots == wanted), touch, 1, 1)
    any_touch = jnp.max(block_touch, axis=0, keepdims=True)
    any_touch = jnp.broadcast_to(any_touch, (8, reqs))
    place = dot(any_touch.astype(BF), before)
    served = (core ^ (lax.shift_right_logical(iota((8, reqs), 1), 2) & 1)) + offset
    in_group = ones_where(lax.shift_right_logical(iota((reqs, 128), 0), 2) == iota((reqs, 128), 1))
    bits = dot(jnp.where(place == served.astype(F32), block_touch, 0.0).astype(BF), in_group)
    most = dot(chip_touch.astype(BF), in_group)
    most = jnp.max(jnp.max(most, axis=0, keepdims=True), axis=1, keepdims=True)
    table_ref[...] = jnp.where(iota((8, 128), 0) == 7, most, bits).astype(jnp.int32)
    for copy in copies:
        copy.wait()


def route(offset, me, q_rows, touch_mask, block_slot):
    n = DEVS * ROWS
    vmem = pl.BlockSpec(memory_space=pltpu.VMEM)
    return pl.pallas_call(
        functools.partial(route_kernel, offset),
        out_shape=(
            jax.ShapeDtypeStruct((n, DK), BF),
            jax.ShapeDtypeStruct((n, 32), BF),
            jax.ShapeDtypeStruct((8, 128), jnp.int32),
        ),
        in_specs=[pl.BlockSpec(memory_space=pltpu.SMEM), vmem, vmem, vmem],
        out_specs=(pl.BlockSpec(memory_space=pl.ANY), vmem, vmem),
        scratch_shapes=[pltpu.VMEM((n, DK), BF), pltpu.SemaphoreType.DMA((4,))],
        compiler_params=pltpu.CompilerParams(vmem_limit_bytes=32 * MIB),
        cost_estimate=pl.CostEstimate(flops=2 * n * 32 * 1024, bytes_accessed=2 * n * DK, transcendentals=0),
        name="route",
    )(me, q_rows, touch_mask, block_slot.reshape(1, -1))


LOG2_E = 1.4426950408889634
LN_2 = 0.6931471805599453


def holder_kernel(table_ref, q_ref, own_ref, peer_ref, out_ref, top, total, acc, out, todo, out_sems):
    counts = []
    for b in range(4):
        count = jnp.int32(0)
        for g in range(GROUPS):
            todo[b, count] = g
            count = count + jnp.where(table_ref[b, g] > 0, 1, 0)
        todo[b, count] = GROUPS
        counts.append(count)
    top[...] = jnp.full(top.shape, MASKED_SCORE, F32)
    total[...] = jnp.ones(total.shape, F32)
    acc[...] = jnp.zeros(acc.shape, F32)
    for b in range(4):
        keys = (own_ref if b < 2 else peer_ref).at[b & 1]

        def step(i, carry, b=b, keys=keys):
            pair = [todo[b, 2 * i], todo[b, 2 * i + 1]]
            rows = jnp.concatenate([q_ref[pair[0]], q_ref[jnp.minimum(pair[1], GROUPS - 1)]], axis=0)
            s = dot(rows, keys[...]) * (SOFTMAX_SCALE * LOG2_E)
            old = jnp.concatenate([top[g] for g in pair], axis=0)
            new = jnp.maximum(old, jnp.max(s, axis=1, keepdims=True))
            scale = jnp.exp2(old - new)
            p = jnp.exp2(s - new)
            added = jnp.sum(p, axis=1, keepdims=True)
            value = dot(p.astype(BF), keys[:LAT, :], 1, 1)
            for k, g in enumerate(pair):
                here = slice(k * GROUP_ROWS, (k + 1) * GROUP_ROWS)
                top[g] = new[here]
                total[g] = total[g] * scale[here] + added[here]
                acc[g] = acc[g] * scale[here] + value[here]
            return carry

        lax.fori_loop(0, lax.shift_right_logical(counts[b] + 1, 1), step, 0)

    copies = []
    for g in range(GROUPS):
        out[g, :, :LAT] = (acc[g] * (1.0 / total[g])).astype(BF)
        lse = (top[g] + jnp.log2(total[g])) * LN_2
        high = lse.astype(BF).astype(F32)
        middle = (lse - high).astype(BF).astype(F32)
        low = lse - high - middle
        lane = iota((GROUP_ROWS, PACK - LAT), 1)
        tail = jnp.where(lane == 0, high, 0.0)
        tail = jnp.where(lane == 1, middle, tail)
        tail = jnp.where(lane == 2, low, tail)
        tail = jnp.where(lane == 3, 1.0, tail)
        out[g, :, LAT:] = tail.astype(BF)
        copies.append(pltpu.make_async_copy(out.at[g], out_ref.at[g], out_sems.at[g]))
        copies[-1].start()
    for copy in copies:
        copy.wait()


def holder(table, queries, own, peer):
    vmem = pl.BlockSpec(memory_space=pltpu.VMEM)
    return pl.pallas_call(
        holder_kernel,
        out_shape=jax.ShapeDtypeStruct((GROUPS, GROUP_ROWS, PACK), BF),
        in_specs=[pl.BlockSpec(memory_space=pltpu.SMEM), vmem, vmem, vmem],
        out_specs=pl.BlockSpec(memory_space=pl.ANY),
        scratch_shapes=[
            pltpu.VMEM((GROUPS + 1, GROUP_ROWS, 1), F32),
            pltpu.VMEM((GROUPS + 1, GROUP_ROWS, 1), F32),
            pltpu.VMEM((GROUPS + 1, GROUP_ROWS, LAT), F32),
            pltpu.VMEM((GROUPS, GROUP_ROWS, PACK), BF),
            pltpu.SMEM((4, 16), jnp.int32),
            pltpu.SemaphoreType.DMA((GROUPS,)),
        ],
        compiler_params=pltpu.CompilerParams(vmem_limit_bytes=32 * MIB),
        cost_estimate=pl.CostEstimate(
            flops=2 * 1024 * 1024 * (DK + LAT), bytes_accessed=4 * 2 * BLK * DK, transcendentals=1024 * 1024
        ),
        name="holder",
    )(table, queries, own, peer)


def suffix_kernel(len_ref, q_ref, kv_ref, out_ref, lse_ref):
    r = pl.program_id(0)
    kv = kv_ref[0]
    s = dot(q_ref[0], kv) * SOFTMAX_SCALE
    s = jnp.where(iota(s.shape, 1) < len_ref[r], s, MASKED_SCORE)
    top = jnp.max(s, axis=1, keepdims=True)
    p = jnp.exp(s - top)
    total = jnp.sum(p, axis=1, keepdims=True)
    out_ref[0] = dot(p.astype(BF), kv[:LAT], 1, 1) / total
    lse_ref[0] = jnp.broadcast_to(top + jnp.log(total), lse_ref.shape[1:])


def suffix(lengths, queries, cache):
    reqs, heads, _ = queries.shape
    return pl.pallas_call(
        suffix_kernel,
        grid=(reqs,),
        out_shape=(
            jax.ShapeDtypeStruct((reqs, heads, LAT), F32),
            jax.ShapeDtypeStruct((reqs, heads, 128), F32),
        ),
        in_specs=[
            pl.BlockSpec(memory_space=pltpu.SMEM),
            pl.BlockSpec((1, heads, DK), lambda r: (r, 0, 0)),
            pl.BlockSpec((1, DK, SUF), lambda r: (r, 0, 0)),
        ],
        out_specs=(
            pl.BlockSpec((1, heads, LAT), lambda r: (r, 0, 0)),
            pl.BlockSpec((1, heads, 128), lambda r: (r, 0, 0)),
        ),
        compiler_params=pltpu.CompilerParams(vmem_limit_bytes=32 * MIB),
        cost_estimate=pl.CostEstimate(
            flops=2 * 4 * 256 * 1024 * (DK + LAT), bytes_accessed=4 * 2 * SUF * DK, transcendentals=4 * 8 * 1024
        ),
        name="suffix",
    )(lengths, queries, cache)


def merge_kernel(rounds, *refs):
    parts, routes = refs[:rounds], refs[rounds : 2 * rounds]
    suffix_ref, suffix_lse_ref, out_ref, lse_ref = refs[2 * rounds :]
    heads = 32
    eye = iota((heads, heads), 0) == iota((heads, heads), 1)
    suffix_lse = suffix_lse_ref[:, :1]
    ceiling = jnp.max(jnp.where(eye, suffix_lse, MASKED_SCORE), axis=0, keepdims=True)
    scores = []
    for part, chosen in zip(parts, routes):
        tail = part[:, LAT:].astype(F32)
        lse = tail[:, 0:1] + tail[:, 1:2] + tail[:, 2:3]
        score = jnp.where(chosen[...] > 0.5, lse, MASKED_SCORE)
        scores.append(score)
        ceiling = jnp.maximum(ceiling, jnp.max(score, axis=0, keepdims=True))
    top = jnp.max(jnp.where(eye, ceiling, MASKED_SCORE), axis=1, keepdims=True)
    weight = jnp.exp(suffix_lse - top)
    merged = weight * suffix_ref[...]
    total = weight
    for part, score in zip(parts, scores):
        w = jnp.exp(score - ceiling)
        high = w.astype(BF)
        low = (w - high.astype(F32)).astype(BF)
        both = jnp.concatenate([high, low], axis=1).T
        sums = dot(both, part[...])
        sums = sums[:heads] + sums[heads:]
        merged = merged + sums[:, :LAT]
        total = total + sums[:, LAT + 3 : LAT + 4]
    out = (merged / total).astype(BF)
    lse = top + jnp.log(total)
    diagonal = iota((8, 8), 0) == iota((8, 8), 1)
    for q in range(4):
        out_ref[q] = out[q * 8 : q * 8 + 8]
        column = jnp.where(diagonal, lse[q * 8 : q * 8 + 8], 0.0)
        lse_ref[q : q + 1, :] = jnp.sum(column, axis=0, keepdims=True)


def merge(parts, routes, suffix_out, suffix_lse):
    vmem = pl.BlockSpec(memory_space=pltpu.VMEM)
    return pl.pallas_call(
        functools.partial(merge_kernel, len(parts)),
        out_shape=(jax.ShapeDtypeStruct((4, 8, LAT), BF), jax.ShapeDtypeStruct((4, 8), F32)),
        in_specs=[vmem] * (2 * len(parts) + 2),
        out_specs=(vmem, vmem),
        compiler_params=pltpu.CompilerParams(vmem_limit_bytes=32 * MIB),
        name="merge",
    )(*parts, *routes, suffix_out, suffix_lse)


AXES = ("z", "core", "x", "y")


def on_device(queries, prefix_cache, suffix_cache, suffix_len, touch_mask, block_slot):
    reqs, heads, _ = queries.shape
    me = lax.axis_index(AXES).astype(jnp.int32).reshape(1)
    q_rows = queries.reshape(reqs * heads, DK)
    own = prefix_cache.transpose(0, 2, 1)
    peer = lax.ppermute(own, "core", [(0, 1), (1, 0)])

    def one_round(offset, peer):
        send, chosen, table = route(offset, me, q_rows, touch_mask, block_slot)
        got = lax.all_to_all(send.reshape(DEVS, ROWS, DK), AXES, split_axis=0, concat_axis=0, tiled=True)
        parts = holder(table, got.reshape(GROUPS, GROUP_ROWS, DK), own, peer)
        parts = lax.all_to_all(parts.reshape(DEVS, ROWS, PACK), AXES, split_axis=0, concat_axis=0, tiled=True)
        return parts.reshape(DEVS * ROWS, PACK), chosen, table

    parts, chosen, table = one_round(0, peer)
    suffix_out, suffix_lse = suffix(suffix_len, queries, suffix_cache.transpose(0, 2, 1))
    suffix_out = suffix_out.reshape(reqs * heads, LAT)
    suffix_lse = suffix_lse.reshape(reqs * heads, 128)

    def one(parts, chosen, peer):
        return merge([parts], [chosen], suffix_out, suffix_lse)

    def two(parts, chosen, peer):
        more, more_chosen, _ = one_round(2, peer)
        return merge([parts, more], [chosen, more_chosen], suffix_out, suffix_lse)

    return tuple(lax.cond(table[7, 0] > 2, two, one, parts, chosen, peer))


def solution(mesh):
    grid = Mesh(mesh.devices.reshape(4, 2, 4, 4), AXES)
    rows, cache = ("z", "core"), ("x", "y")
    in_specs = (
        P(rows, cache, None),
        P(AXES, None, None),
        P(rows, None, None),
        P(rows),
        P(),
        P(),
    )
    out_specs = (P(rows, cache, None), P(rows, cache))
    return jax.shard_map(
        on_device, mesh=grid, in_specs=in_specs, out_specs=out_specs, check_vma=False
    )
```

```python
import functools
import jax
import jax.numpy as jnp
from jax import lax
from jax.experimental import pallas as pl
from jax.experimental.pallas import tpu as pltpu
from jax.sharding import Mesh, PartitionSpec as P

H = 128
LAT = 512
DK = 576
BLK = 1024
BLK_DEV = 2
SUF = 1024
DEVS = 128
ROWS = 8
PACK = 640
GROUPS = 8
GROUP_ROWS = 128
PARTS = 1

SOFTMAX_SCALE = 192.0 ** (-0.5)
MASKED_SCORE = -1e30
BF = jnp.bfloat16
F32 = jnp.float32
MIB = 1024 * 1024


def iota(shape, dim):
    return lax.broadcasted_iota(jnp.int32, shape, dim)


def ones_where(mask):
    return jnp.where(mask, 1.0, 0.0).astype(BF)


def dot(a, b, ca=1, cb=0):
    return lax.dot_general(a, b, (((ca,), (cb,)), ((), ())), preferred_element_type=F32)


def route_kernel(offset, me_ref, q_ref, touch_ref, slot_ref, send_ref, route_ref, table_ref, picked, stage, sems):
    me = me_ref[0]
    group = lax.shift_right_logical(me, 4)
    n = DEVS * ROWS
    chips = DEVS // 2
    touch = touch_ref[...].astype(F32).astype(BF)
    reqs, blocks = touch.shape
    slots = slot_ref[...]
    chip_of = lax.shift_right_logical(slots, 6) * 16 + (lax.shift_right_logical(slots, 1) & 15)
    chip_touch = dot(ones_where(iota((chips, blocks), 0) == chip_of), touch, 1, 1)
    chip_touch = jnp.minimum(chip_touch, 1.0)
    of_group = lax.shift_right_logical(iota((reqs, reqs), 0), 2)
    before = ones_where(
        (of_group == lax.shift_right_logical(iota((reqs, reqs), 1), 2)) & (iota((reqs, reqs), 0) < iota((reqs, reqs), 1))
    )
    rank = dot(chip_touch.astype(BF), before)
    mine = ones_where(iota((reqs, 32), 0) == group * 4 + lax.shift_right_logical(iota((reqs, 32), 1), 3))
    first = ((group & 1) + offset).astype(F32)
    second = ((1 - (group & 1)) + offset).astype(F32)
    by_core = [jnp.where(rank == want, chip_touch, 0.0) for want in (first, second)]
    by_dev = [by_core[k][z * 16 : z * 16 + 16] for z in range(4) for k in (0, 1)]
    by_dev = dot(jnp.concatenate(by_dev, axis=0).astype(BF), mine)
    part = n // PARTS

    def copy(i):
        here = pl.ds(i * part, part)
        return pltpu.make_async_copy(stage.at[here], send_ref.at[here], sems.at[i])

    def fill(i, carry):
        here = pl.ds(i * part, part)
        chosen = by_dev[i * (part // ROWS) : (i + 1) * (part // ROWS)]
        chosen = jnp.broadcast_to(chosen[:, None, :], (part // ROWS, ROWS, 32)).reshape(part, 32)
        chosen = jnp.where((iota((part, 32), 1) & 7) == (iota((part, 32), 0) & 7), chosen, 0.0).astype(BF)
        route_ref[here, :] = chosen
        stage[here, :] = dot(chosen, q_ref[...]).astype(BF)
        copy(i).start()
        return carry

    for i in range(PARTS):
        fill(i, 0)
    @pl.when(me >= 0)
    def _():
        core = lax.shift_right_logical(me, 4) & 1
        b = iota((8, blocks), 0)
        owner = jnp.where(b < 2, me, me ^ 16)
        wanted = jnp.where(b < 4, owner * 2 + (b & 1), -1)
        block_touch = dot(ones_where(slots == wanted), touch, 1, 1)
        any_touch = jnp.max(block_touch, axis=0, keepdims=True)
        any_touch = jnp.broadcast_to(any_touch, (8, reqs))
        place = dot(any_touch.astype(BF), before)
        served = (core ^ (lax.shift_right_logical(iota((8, reqs), 1), 2) & 1)) + offset
        in_group = ones_where(lax.shift_right_logical(iota((reqs, 128), 0), 2) == iota((reqs, 128), 1))
        bits = dot(jnp.where(place == served.astype(F32), block_touch, 0.0).astype(BF), in_group)
        most = dot(chip_touch.astype(BF), in_group)
        most = jnp.max(jnp.max(most, axis=0, keepdims=True), axis=1, keepdims=True)
        table_ref[...] = jnp.where(iota((8, 128), 0) == 7, most, bits).astype(jnp.int32)

    for i in range(PARTS):
        copy(i).wait()


def route(offset, me, q_rows, touch_mask, block_slot):
    n = DEVS * ROWS
    vmem = pl.BlockSpec(memory_space=pltpu.VMEM)
    return pl.pallas_call(
        functools.partial(route_kernel, offset),
        out_shape=(
            jax.ShapeDtypeStruct((n, DK), BF),
            jax.ShapeDtypeStruct((n, 32), BF),
            jax.ShapeDtypeStruct((8, 128), jnp.int32),
        ),
        in_specs=[pl.BlockSpec(memory_space=pltpu.SMEM), vmem, vmem, vmem],
        out_specs=(pl.BlockSpec(memory_space=pl.ANY), vmem, vmem),
        scratch_shapes=[pltpu.VMEM((DEVS, 32), F32), pltpu.VMEM((n, DK), BF), pltpu.SemaphoreType.DMA((PARTS,))],
        compiler_params=pltpu.CompilerParams(vmem_limit_bytes=32 * MIB),
        cost_estimate=pl.CostEstimate(flops=2 * n * 32 * 1024, bytes_accessed=2 * n * DK, transcendentals=0),
        name="route",
    )(me, q_rows, touch_mask, block_slot.reshape(1, -1))


LOG2_E = 1.4426950408889634
LN_2 = 0.6931471805599453


def holder_kernel(table_ref, q_ref, own_ref, peer_ref, out_ref, top, total, acc, out, todo, out_sems):
    counts = []
    for b in range(4):
        count = jnp.int32(0)
        for g in range(GROUPS):
            todo[b, count] = g
            count = count + jnp.where(table_ref[b, g] > 0, 1, 0)
        todo[b, count] = GROUPS
        counts.append(count)
    top[...] = jnp.full(top.shape, MASKED_SCORE, F32)
    total[...] = jnp.ones(total.shape, F32)
    acc[...] = jnp.zeros(acc.shape, F32)
    def work(ref, units):
        c = SOFTMAX_SCALE * LOG2_E
        scores = []
        for block, pair in units:
            rows = jnp.concatenate([q_ref[jnp.minimum(g, GROUPS - 1)] for g in pair], axis=0)
            scores.append(dot(rows, ref[block]))
        for s, (block, pair) in zip(scores, units):
            old = jnp.concatenate([top[g] for g in pair], axis=0)
            new = jnp.maximum(old, jnp.max(s, axis=1, keepdims=True) * c)
            scale = jnp.exp2(old - new)
            p = jnp.exp2(s * c - new)
            added = jnp.sum(p, axis=1, keepdims=True)
            value = dot(p.astype(BF), ref[block, :LAT, :], 1, 1)
            for k, g in enumerate(pair):
                here = slice(k * GROUP_ROWS, (k + 1) * GROUP_ROWS)
                top[g] = new[here]
                total[g] = total[g] * scale[here] + added[here]
                acc[g] = acc[g] * scale[here] + value[here]

    for half, ref in enumerate((own_ref, peer_ref)):
        pairs = [lax.shift_right_logical(counts[2 * half + k] + 1, 1) for k in (0, 1)]
        n = pairs[0] + pairs[1]

        def unit(u, half=half, pairs=pairs):
            block = jnp.where(u < pairs[0], 0, 1)
            i = 2 * (u - block * pairs[0])
            return block, [todo[2 * half + block, i], todo[2 * half + block, i + 1]]

        def step(i, carry, ref=ref, unit=unit):
            work(ref, [unit(2 * i), unit(2 * i + 1)])
            return carry

        lax.fori_loop(0, lax.shift_right_logical(n, 1), step, 0)

        @pl.when((n & 1) == 1)
        def _(ref=ref, unit=unit, n=n):
            work(ref, [unit(n - 1)])

    copies = []
    for g in range(GROUPS):
        out[g, :, :LAT] = (acc[g] * (1.0 / total[g])).astype(BF)
        lse = (top[g] + jnp.log2(total[g])) * LN_2
        high = lse.astype(BF).astype(F32)
        middle = (lse - high).astype(BF).astype(F32)
        low = lse - high - middle
        lane = iota((GROUP_ROWS, PACK - LAT), 1)
        tail = jnp.where(lane == 0, high, 0.0)
        tail = jnp.where(lane == 1, middle, tail)
        tail = jnp.where(lane == 2, low, tail)
        tail = jnp.where(lane == 3, 1.0, tail)
        out[g, :, LAT:] = tail.astype(BF)
        copies.append(pltpu.make_async_copy(out.at[g], out_ref.at[g], out_sems.at[g]))
        copies[-1].start()
    for copy in copies:
        copy.wait()


def holder(table, queries, own, peer):
    vmem = pl.BlockSpec(memory_space=pltpu.VMEM)
    return pl.pallas_call(
        holder_kernel,
        out_shape=jax.ShapeDtypeStruct((GROUPS, GROUP_ROWS, PACK), BF),
        in_specs=[pl.BlockSpec(memory_space=pltpu.SMEM), vmem, vmem, vmem],
        out_specs=pl.BlockSpec(memory_space=pl.ANY),
        scratch_shapes=[
            pltpu.VMEM((GROUPS + 1, GROUP_ROWS, 1), F32),
            pltpu.VMEM((GROUPS + 1, GROUP_ROWS, 1), F32),
            pltpu.VMEM((GROUPS + 1, GROUP_ROWS, LAT), F32),
            pltpu.VMEM((GROUPS, GROUP_ROWS, PACK), BF),
            pltpu.SMEM((4, 16), jnp.int32),
            pltpu.SemaphoreType.DMA((GROUPS,)),
        ],
        compiler_params=pltpu.CompilerParams(vmem_limit_bytes=32 * MIB),
        cost_estimate=pl.CostEstimate(
            flops=2 * 1024 * 1024 * (DK + LAT), bytes_accessed=4 * 2 * BLK * DK, transcendentals=1024 * 1024
        ),
        name="holder",
    )(table, queries, own, peer)


def suffix_kernel(len_ref, q_ref, kv_ref, out_ref, lse_ref):
    r = pl.program_id(0)
    kv = kv_ref[0]
    s = dot(q_ref[0], kv) * SOFTMAX_SCALE
    s = jnp.where(iota(s.shape, 1) < len_ref[r], s, MASKED_SCORE)
    top = jnp.max(s, axis=1, keepdims=True)
    p = jnp.exp(s - top)
    total = jnp.sum(p, axis=1, keepdims=True)
    out_ref[0] = dot(p.astype(BF), kv[:LAT], 1, 1) / total
    lse_ref[0] = jnp.broadcast_to(top + jnp.log(total), lse_ref.shape[1:])


def suffix(lengths, queries, cache):
    reqs, heads, _ = queries.shape
    return pl.pallas_call(
        suffix_kernel,
        grid=(reqs,),
        out_shape=(
            jax.ShapeDtypeStruct((reqs, heads, LAT), F32),
            jax.ShapeDtypeStruct((reqs, heads, 128), F32),
        ),
        in_specs=[
            pl.BlockSpec(memory_space=pltpu.SMEM),
            pl.BlockSpec((1, heads, DK), lambda r: (r, 0, 0)),
            pl.BlockSpec((1, DK, SUF), lambda r: (r, 0, 0)),
        ],
        out_specs=(
            pl.BlockSpec((1, heads, LAT), lambda r: (r, 0, 0)),
            pl.BlockSpec((1, heads, 128), lambda r: (r, 0, 0)),
        ),
        compiler_params=pltpu.CompilerParams(vmem_limit_bytes=32 * MIB),
        cost_estimate=pl.CostEstimate(
            flops=2 * 4 * 256 * 1024 * (DK + LAT), bytes_accessed=4 * 2 * SUF * DK, transcendentals=4 * 8 * 1024
        ),
        name="suffix",
    )(lengths, queries, cache)


def merge_kernel(rounds, *refs):
    parts, routes = refs[:rounds], refs[rounds : 2 * rounds]
    suffix_ref, suffix_lse_ref, out_ref, lse_ref = refs[2 * rounds :]
    heads = 32
    eye = iota((heads, heads), 0) == iota((heads, heads), 1)
    suffix_lse = suffix_lse_ref[:, :1]
    ceiling = jnp.max(jnp.where(eye, suffix_lse, MASKED_SCORE), axis=0, keepdims=True)
    scores = []
    for part, chosen in zip(parts, routes):
        tail = part[:, LAT:].astype(F32)
        lse = tail[:, 0:1] + tail[:, 1:2] + tail[:, 2:3]
        score = jnp.where(chosen[...] > 0.5, lse, MASKED_SCORE)
        scores.append(score)
        ceiling = jnp.maximum(ceiling, jnp.max(score, axis=0, keepdims=True))
    top = jnp.max(jnp.where(eye, ceiling, MASKED_SCORE), axis=1, keepdims=True)
    weight = jnp.exp(suffix_lse - top)
    merged = weight * suffix_ref[...]
    total = weight
    for part, score in zip(parts, scores):
        w = jnp.exp(score - ceiling)
        high = w.astype(BF)
        low = (w - high.astype(F32)).astype(BF)
        both = jnp.concatenate([high, low], axis=1).T
        sums = dot(both, part[...])
        sums = sums[:heads] + sums[heads:]
        merged = merged + sums[:, :LAT]
        total = total + sums[:, LAT + 3 : LAT + 4]
    out = (merged / total).astype(BF)
    lse = top + jnp.log(total)
    diagonal = iota((8, 8), 0) == iota((8, 8), 1)
    for q in range(4):
        out_ref[q] = out[q * 8 : q * 8 + 8]
        column = jnp.where(diagonal, lse[q * 8 : q * 8 + 8], 0.0)
        lse_ref[q : q + 1, :] = jnp.sum(column, axis=0, keepdims=True)


def merge(parts, routes, suffix_out, suffix_lse):
    vmem = pl.BlockSpec(memory_space=pltpu.VMEM)
    return pl.pallas_call(
        functools.partial(merge_kernel, len(parts)),
        out_shape=(jax.ShapeDtypeStruct((4, 8, LAT), BF), jax.ShapeDtypeStruct((4, 8), F32)),
        in_specs=[vmem] * (2 * len(parts) + 2),
        out_specs=(vmem, vmem),
        compiler_params=pltpu.CompilerParams(vmem_limit_bytes=32 * MIB),
        name="merge",
    )(*parts, *routes, suffix_out, suffix_lse)


AXES = ("z", "core", "x", "y")


def on_device(queries, prefix_cache, suffix_cache, suffix_len, touch_mask, block_slot):
    reqs, heads, _ = queries.shape
    me = lax.axis_index(AXES).astype(jnp.int32).reshape(1)
    q_rows = queries.reshape(reqs * heads, DK)
    own = prefix_cache.transpose(0, 2, 1)
    peer = lax.ppermute(own, "core", [(0, 1), (1, 0)])

    def one_round(offset, peer):
        send, chosen, table = route(offset, me, q_rows, touch_mask, block_slot)
        got = lax.all_to_all(send.reshape(DEVS, ROWS, DK), AXES, split_axis=0, concat_axis=0, tiled=True)
        parts = holder(table, got.reshape(GROUPS, GROUP_ROWS, DK), own, peer)
        parts = lax.all_to_all(parts.reshape(DEVS, ROWS, PACK), AXES, split_axis=0, concat_axis=0, tiled=True)
        return parts.reshape(DEVS * ROWS, PACK), chosen, table

    parts, chosen, table = one_round(0, peer)
    suffix_out, suffix_lse = suffix(suffix_len, queries, suffix_cache.transpose(0, 2, 1))
    suffix_out = suffix_out.reshape(reqs * heads, LAT)
    suffix_lse = suffix_lse.reshape(reqs * heads, 128)

    def one(parts, chosen, peer):
        return merge([parts], [chosen], suffix_out, suffix_lse)

    def two(parts, chosen, peer):
        more, more_chosen, _ = one_round(2, peer)
        return merge([parts, more], [chosen, more_chosen], suffix_out, suffix_lse)

    return tuple(lax.cond(table[7, 0] > 2, two, one, parts, chosen, peer))


def solution(mesh):
    grid = Mesh(mesh.devices.reshape(4, 2, 4, 4), AXES)
    rows, cache = ("z", "core"), ("x", "y")
    in_specs = (
        P(rows, cache, None),
        P(AXES, None, None),
        P(rows, None, None),
        P(rows),
        P(),
        P(),
    )
    out_specs = (P(rows, cache, None), P(rows, cache))
    return jax.shard_map(
        on_device, mesh=grid, in_specs=in_specs, out_specs=out_specs, check_vma=False
    )
```

```python
import functools
import jax
import jax.numpy as jnp
from jax import lax
from jax.experimental import pallas as pl
from jax.experimental.pallas import tpu as pltpu
from jax.sharding import Mesh, PartitionSpec as P

H = 128
LAT = 512
DK = 576
BLK = 1024
BLK_DEV = 2
SUF = 1024
DEVS = 128
SIDE = 2
ROWS = 8 // SIDE
SEND = SIDE * DK
PACK = SIDE * LAT + 128
GROUPS = 8
GROUP_ROWS = 128

SOFTMAX_SCALE = 192.0 ** (-0.5)
MASKED_SCORE = -1e30
BF = jnp.bfloat16
F32 = jnp.float32
MIB = 1024 * 1024


def iota(shape, dim):
    return lax.broadcasted_iota(jnp.int32, shape, dim)


def ones_where(mask):
    return jnp.where(mask, 1.0, 0.0).astype(BF)


def dot(a, b, ca=1, cb=0):
    return lax.dot_general(a, b, (((ca,), (cb,)), ((), ())), preferred_element_type=F32)


def route_kernel(offset, me_ref, q_ref, touch_ref, slot_ref, send_ref, route_ref, table_ref):
    me = me_ref[0]
    group = lax.shift_right_logical(me, 4)
    n = DEVS * ROWS
    chips = DEVS // 2
    touch = touch_ref[...].astype(F32).astype(BF)
    reqs, blocks = touch.shape
    slots = slot_ref[...]
    chip_of = lax.shift_right_logical(slots, 6) * 16 + (lax.shift_right_logical(slots, 1) & 15)
    chip_touch = dot(ones_where(iota((chips, blocks), 0) == chip_of), touch, 1, 1)
    chip_touch = jnp.minimum(chip_touch, 1.0)
    of_group = lax.shift_right_logical(iota((reqs, reqs), 0), 2)
    before = ones_where(
        (of_group == lax.shift_right_logical(iota((reqs, reqs), 1), 2)) & (iota((reqs, reqs), 0) < iota((reqs, reqs), 1))
    )
    rank = dot(chip_touch.astype(BF), before)
    mine = ones_where(iota((reqs, 32), 0) == group * 4 + lax.shift_right_logical(iota((reqs, 32), 1), 3))
    first = ((group & 1) + offset).astype(F32)
    second = ((1 - (group & 1)) + offset).astype(F32)
    by_core = [jnp.where(rank == want, chip_touch, 0.0) for want in (first, second)]
    by_dev = [by_core[k][z * 16 : z * 16 + 16] for z in range(4) for k in (0, 1)]
    by_dev = dot(jnp.concatenate(by_dev, axis=0).astype(BF), mine)
    chosen = jnp.broadcast_to(by_dev[:, None, :], (DEVS, ROWS, 32)).reshape(n, 32)
    in_row = (iota((n, 32), 1) & 7) // SIDE == (iota((n, 32), 0) & (ROWS - 1))
    chosen = jnp.where(in_row, chosen, 0.0)
    route_ref[...] = chosen.astype(BF)
    by_place, spread = [], []
    q = q_ref[...].astype(F32)
    for j in range(SIDE):
        by_place.append(jnp.where((iota((n, 32), 1) & (SIDE - 1)) == j, chosen, 0.0))
        pieces = [jnp.zeros((32, j * LAT), F32), q[:, :LAT], jnp.zeros((32, (SIDE - 1 - j) * LAT), F32)]
        pieces += [jnp.zeros((32, j * (DK - LAT)), F32), q[:, LAT:], jnp.zeros((32, (SIDE - 1 - j) * (DK - LAT)), F32)]
        spread.append(jnp.concatenate([piece for piece in pieces if piece.shape[1]], axis=1))
    by_place = jnp.concatenate(by_place, axis=1).astype(BF)
    spread = jnp.concatenate(spread, axis=0).astype(BF)
    send_ref[...] = dot(by_place, spread).astype(BF).reshape(send_ref.shape)
    core = lax.shift_right_logical(me, 4) & 1
    b = iota((8, blocks), 0)
    owner = jnp.where(b < 2, me, me ^ 16)
    wanted = jnp.where(b < 4, owner * 2 + (b & 1), -1)
    block_touch = dot(ones_where(slots == wanted), touch, 1, 1)
    any_touch = jnp.max(block_touch, axis=0, keepdims=True)
    any_touch = jnp.broadcast_to(any_touch, (8, reqs))
    place = dot(any_touch.astype(BF), before)
    served = (core ^ (lax.shift_right_logical(iota((8, reqs), 1), 2) & 1)) + offset
    in_group = ones_where(lax.shift_right_logical(iota((reqs, 128), 0), 2) == iota((reqs, 128), 1))
    bits = dot(jnp.where(place == served.astype(F32), block_touch, 0.0).astype(BF), in_group)
    most = dot(chip_touch.astype(BF), in_group)
    most = jnp.max(jnp.max(most, axis=0, keepdims=True), axis=1, keepdims=True)
    table_ref[...] = jnp.where(iota((8, 128), 0) == 7, most, bits).astype(jnp.int32)


def route(offset, me, q_rows, touch_mask, block_slot):
    n = DEVS * ROWS
    vmem = pl.BlockSpec(memory_space=pltpu.VMEM)
    return pl.pallas_call(
        functools.partial(route_kernel, offset),
        out_shape=(
            jax.ShapeDtypeStruct((DEVS, ROWS, SEND), BF),
            jax.ShapeDtypeStruct((n, 32), BF),
            jax.ShapeDtypeStruct((8, 128), jnp.int32),
        ),
        in_specs=[pl.BlockSpec(memory_space=pltpu.SMEM), vmem, vmem, vmem],
        out_specs=(vmem, vmem, vmem),
        compiler_params=pltpu.CompilerParams(vmem_limit_bytes=32 * MIB),
        cost_estimate=pl.CostEstimate(flops=2 * n * 32 * 1024, bytes_accessed=2 * n * SEND, transcendentals=0),
        name="route",
    )(me, q_rows, touch_mask, block_slot.reshape(1, -1))


LOG2_E = 1.4426950408889634
LN_2 = 0.6931471805599453


def holder_kernel(table_ref, packets_ref, own_ref, far_ref, out_ref, peer_ref, q, top, total, acc, out, todo, out_sems, peer_sem):
    fetch = pltpu.make_async_copy(far_ref, peer_ref, peer_sem)
    fetch.start()
    share = 16 * ROWS
    for g in range(GROUPS):
        x = packets_ref[g * 16 : g * 16 + 16].reshape(share, SEND)
        for j in range(SIDE):
            here = slice(j * share, j * share + share)
            q[g, here, :LAT] = x[:, j * LAT : j * LAT + LAT]
            rotary = SIDE * LAT + j * (DK - LAT)
            q[g, here, LAT:] = x[:, rotary : rotary + DK - LAT]
    counts = []
    for b in range(4):
        count = jnp.int32(0)
        for g in range(GROUPS):
            todo[b, count] = g
            count = count + jnp.where(table_ref[b, g] > 0, 1, 0)
        todo[b, count] = GROUPS
        counts.append(count)
    top[...] = jnp.full(top.shape, MASKED_SCORE, F32)
    total[...] = jnp.ones(total.shape, F32)
    acc[...] = jnp.zeros(acc.shape, F32)
    def work(ref, units):
        c = SOFTMAX_SCALE * LOG2_E
        scores = []
        for block, pair in units:
            rows = jnp.concatenate([q[jnp.minimum(g, GROUPS - 1)] for g in pair], axis=0)
            scores.append(dot(rows, ref[block]))
        for s, (block, pair) in zip(scores, units):
            old = jnp.concatenate([top[g] for g in pair], axis=0)
            new = jnp.maximum(old, jnp.max(s, axis=1, keepdims=True) * c)
            scale = jnp.exp2(old - new)
            p = jnp.exp2(s * c - new)
            added = jnp.sum(p, axis=1, keepdims=True)
            value = dot(p.astype(BF), ref[block, :LAT, :], 1, 1)
            for k, g in enumerate(pair):
                here = slice(k * GROUP_ROWS, (k + 1) * GROUP_ROWS)
                top[g] = new[here]
                total[g] = total[g] * scale[here] + added[here]
                acc[g] = acc[g] * scale[here] + value[here]

    for half, ref in enumerate((own_ref, peer_ref)):
        if half == 1:
            fetch.wait()
        pairs = [lax.shift_right_logical(counts[2 * half + k] + 1, 1) for k in (0, 1)]
        n = pairs[0] + pairs[1]

        def unit(u, half=half, pairs=pairs):
            block = jnp.where(u < pairs[0], 0, 1)
            i = 2 * (u - block * pairs[0])
            return block, [todo[2 * half + block, i], todo[2 * half + block, i + 1]]

        def step(i, carry, ref=ref, unit=unit):
            work(ref, [unit(2 * i), unit(2 * i + 1)])
            return carry

        lax.fori_loop(0, lax.shift_right_logical(n, 1), step, 0)

        @pl.when((n & 1) == 1)
        def _(ref=ref, unit=unit, n=n):
            work(ref, [unit(n - 1)])

    copies = []
    for g in range(GROUPS):
        value = acc[g] * (1.0 / total[g])
        lse = (top[g] + jnp.log2(total[g])) * LN_2
        high = lse.astype(BF).astype(F32)
        middle = (lse - high).astype(BF).astype(F32)
        low = lse - high - middle
        lane = iota((share, 128), 1)
        tail = jnp.where(lane == 3 * SIDE, 1.0, 0.0)
        for j in range(SIDE):
            for k, piece in enumerate((high, middle, low)):
                tail = jnp.where(lane == 3 * j + k, piece[j * share : j * share + share], tail)
        row = [value[j * share : j * share + share] for j in range(SIDE)] + [tail]
        row = jnp.concatenate(row, axis=1).astype(BF)
        here = pl.ds(g * 16, 16)
        out[here] = row.reshape(16, ROWS, PACK)
        copies.append(pltpu.make_async_copy(out.at[here], out_ref.at[here], out_sems.at[g]))
        copies[-1].start()
    for copy in copies:
        copy.wait()


def holder(table, queries, own, peer):
    vmem = pl.BlockSpec(memory_space=pltpu.VMEM)
    return pl.pallas_call(
        holder_kernel,
        out_shape=jax.ShapeDtypeStruct((DEVS, ROWS, PACK), BF),
        in_specs=[pl.BlockSpec(memory_space=pltpu.SMEM), vmem, vmem, pl.BlockSpec(memory_space=pl.ANY)],
        out_specs=pl.BlockSpec(memory_space=pl.ANY),
        scratch_shapes=[
            pltpu.VMEM((BLK_DEV, DK, BLK), BF),
            pltpu.VMEM((GROUPS, GROUP_ROWS, DK), BF),
            pltpu.VMEM((GROUPS + 1, GROUP_ROWS, 1), F32),
            pltpu.VMEM((GROUPS + 1, GROUP_ROWS, 1), F32),
            pltpu.VMEM((GROUPS + 1, GROUP_ROWS, LAT), F32),
            pltpu.VMEM((DEVS, ROWS, PACK), BF),
            pltpu.SMEM((4, 16), jnp.int32),
            pltpu.SemaphoreType.DMA((GROUPS,)),
            pltpu.SemaphoreType.DMA,
        ],
        compiler_params=pltpu.CompilerParams(vmem_limit_bytes=32 * MIB),
        cost_estimate=pl.CostEstimate(
            flops=2 * 1024 * 1024 * (DK + LAT), bytes_accessed=4 * 2 * BLK * DK, transcendentals=1024 * 1024
        ),
        name="holder",
    )(table, queries, own, peer)


def suffix_kernel(len_ref, q_ref, kv_ref, out_ref, lse_ref):
    r = pl.program_id(0)
    kv = kv_ref[0]
    s = dot(q_ref[0], kv) * SOFTMAX_SCALE
    s = jnp.where(iota(s.shape, 1) < len_ref[r], s, MASKED_SCORE)
    top = jnp.max(s, axis=1, keepdims=True)
    p = jnp.exp(s - top)
    total = jnp.sum(p, axis=1, keepdims=True)
    out_ref[0] = dot(p.astype(BF), kv[:LAT], 1, 1) / total
    lse_ref[0] = jnp.broadcast_to(top + jnp.log(total), lse_ref.shape[1:])


def suffix(lengths, queries, cache):
    reqs, heads, _ = queries.shape
    return pl.pallas_call(
        suffix_kernel,
        grid=(reqs,),
        out_shape=(
            jax.ShapeDtypeStruct((reqs, heads, LAT), F32),
            jax.ShapeDtypeStruct((reqs, heads, 128), F32),
        ),
        in_specs=[
            pl.BlockSpec(memory_space=pltpu.SMEM),
            pl.BlockSpec((1, heads, DK), lambda r: (r, 0, 0)),
            pl.BlockSpec((1, DK, SUF), lambda r: (r, 0, 0)),
        ],
        out_specs=(
            pl.BlockSpec((1, heads, LAT), lambda r: (r, 0, 0)),
            pl.BlockSpec((1, heads, 128), lambda r: (r, 0, 0)),
        ),
        compiler_params=pltpu.CompilerParams(vmem_limit_bytes=32 * MIB),
        cost_estimate=pl.CostEstimate(
            flops=2 * 4 * 256 * 1024 * (DK + LAT), bytes_accessed=4 * 2 * SUF * DK, transcendentals=4 * 8 * 1024
        ),
        name="suffix",
    )(lengths, queries, cache)


def merge_kernel(rounds, *refs):
    parts, routes = refs[:rounds], refs[rounds : 2 * rounds]
    suffix_ref, suffix_lse_ref, out_ref, lse_ref = refs[2 * rounds :]
    heads = 32
    eye = iota((heads, heads), 0) == iota((heads, heads), 1)
    suffix_lse = suffix_lse_ref[:, :1]
    ceiling = jnp.max(jnp.where(eye, suffix_lse, MASKED_SCORE), axis=0, keepdims=True)
    scores = []
    n = DEVS * ROWS
    flat = [part[...].reshape(n, PACK) for part in parts]
    place = iota((n, heads), 1) & (SIDE - 1)
    for part, chosen in zip(flat, routes):
        tail = part[:, SIDE * LAT :].astype(F32)
        score = MASKED_SCORE
        for j in range(SIDE):
            lse = tail[:, 3 * j : 3 * j + 1] + tail[:, 3 * j + 1 : 3 * j + 2] + tail[:, 3 * j + 2 : 3 * j + 3]
            score = jnp.where(place == j, lse, score)
        score = jnp.where(chosen[...] > 0.5, score, MASKED_SCORE)
        scores.append(score)
        ceiling = jnp.maximum(ceiling, jnp.max(score, axis=0, keepdims=True))
    top = jnp.max(jnp.where(eye, ceiling, MASKED_SCORE), axis=1, keepdims=True)
    weight = jnp.exp(suffix_lse - top)
    merged = weight * suffix_ref[...]
    total = weight
    place = iota((heads, LAT), 0) & (SIDE - 1)
    for part, score in zip(flat, scores):
        w = jnp.exp(score - ceiling)
        high = w.astype(BF)
        low = (w - high.astype(F32)).astype(BF)
        both = jnp.concatenate([high, low], axis=1).T
        sums = dot(both, part)
        sums = sums[:heads] + sums[heads:]
        total = total + sums[:, SIDE * LAT + 3 * SIDE : SIDE * LAT + 3 * SIDE + 1]
        for j in range(SIDE):
            merged = merged + jnp.where(place == j, sums[:, j * LAT : j * LAT + LAT], 0.0)
    out = (merged / total).astype(BF)
    lse = top + jnp.log(total)
    diagonal = iota((8, 8), 0) == iota((8, 8), 1)
    for q in range(4):
        out_ref[q] = out[q * 8 : q * 8 + 8]
        column = jnp.where(diagonal, lse[q * 8 : q * 8 + 8], 0.0)
        lse_ref[q : q + 1, :] = jnp.sum(column, axis=0, keepdims=True)


def merge(parts, routes, suffix_out, suffix_lse):
    vmem = pl.BlockSpec(memory_space=pltpu.VMEM)
    return pl.pallas_call(
        functools.partial(merge_kernel, len(parts)),
        out_shape=(jax.ShapeDtypeStruct((4, 8, LAT), BF), jax.ShapeDtypeStruct((4, 8), F32)),
        in_specs=[vmem] * (2 * len(parts) + 2),
        out_specs=(vmem, vmem),
        compiler_params=pltpu.CompilerParams(vmem_limit_bytes=32 * MIB),
        name="merge",
    )(*parts, *routes, suffix_out, suffix_lse)


AXES = ("z", "core", "x", "y")


def on_device(queries, prefix_cache, suffix_cache, suffix_len, touch_mask, block_slot):
    reqs, heads, _ = queries.shape
    me = lax.axis_index(AXES).astype(jnp.int32).reshape(1)
    q_rows = queries.reshape(reqs * heads, DK)
    own = prefix_cache.transpose(0, 2, 1)
    peer = lax.ppermute(own, "core", [(0, 1), (1, 0)])

    def one_round(offset, peer):
        send, chosen, table = route(offset, me, q_rows, touch_mask, block_slot)
        got = lax.all_to_all(send, AXES, split_axis=0, concat_axis=0, tiled=True)
        parts = holder(table, got, own, peer)
        parts = lax.all_to_all(parts, AXES, split_axis=0, concat_axis=0, tiled=True)
        return parts, chosen, table

    parts, chosen, table = one_round(0, peer)
    suffix_out, suffix_lse = suffix(suffix_len, queries, suffix_cache.transpose(0, 2, 1))
    suffix_out = suffix_out.reshape(reqs * heads, LAT)
    suffix_lse = suffix_lse.reshape(reqs * heads, 128)

    def one(parts, chosen, peer):
        return merge([parts], [chosen], suffix_out, suffix_lse)

    def two(parts, chosen, peer):
        more, more_chosen, _ = one_round(2, peer)
        return merge([parts, more], [chosen, more_chosen], suffix_out, suffix_lse)

    return tuple(lax.cond(table[7, 0] > 2, two, one, parts, chosen, peer))


def solution(mesh):
    grid = Mesh(mesh.devices.reshape(4, 2, 4, 4), AXES)
    rows, cache = ("z", "core"), ("x", "y")
    in_specs = (
        P(rows, cache, None),
        P(AXES, None, None),
        P(rows, None, None),
        P(rows),
        P(),
        P(),
    )
    out_specs = (P(rows, cache, None), P(rows, cache))
    return jax.shard_map(
        on_device, mesh=grid, in_specs=in_specs, out_specs=out_specs, check_vma=False
    )
```

```python
import functools
import jax
import jax.numpy as jnp
from jax import lax
from jax.experimental import pallas as pl
from jax.experimental.pallas import tpu as pltpu
from jax.sharding import Mesh, PartitionSpec as P

H = 128
LAT = 512
DK = 576
BLK = 1024
BLK_DEV = 2
SUF = 1024
DEVS = 128
SIDE = 2
ROWS = 8 // SIDE
SEND = SIDE * DK
PACK = SIDE * LAT + 128
GROUPS = 8
GROUP_ROWS = 128

SOFTMAX_SCALE = 192.0 ** (-0.5)
MASKED_SCORE = -1e30
BF = jnp.bfloat16
F32 = jnp.float32
MIB = 1024 * 1024


def iota(shape, dim):
    return lax.broadcasted_iota(jnp.int32, shape, dim)


def ones_where(mask):
    return jnp.where(mask, 1.0, 0.0).astype(BF)


def dot(a, b, ca=1, cb=0):
    return lax.dot_general(a, b, (((ca,), (cb,)), ((), ())), preferred_element_type=F32)


def route_kernel(offset, me_ref, q_ref, touch_ref, slot_ref, send_ref, route_ref, table_ref):
    me = me_ref[0]
    group = lax.shift_right_logical(me, 4)
    n = DEVS * ROWS
    chips = DEVS // 2
    touch = touch_ref[...].astype(F32).astype(BF)
    reqs, blocks = touch.shape
    slots = slot_ref[...]
    chip_of = lax.shift_right_logical(slots, 6) * 16 + (lax.shift_right_logical(slots, 1) & 15)
    b = iota((8, blocks), 0)
    wanted = jnp.where(b < 4, jnp.where(b < 2, me, me ^ 16) * 2 + (b & 1), -1)
    rows = [ones_where(iota((chips, blocks), 0) == chip_of), ones_where(slots == wanted)]
    counted = dot(jnp.concatenate(rows, axis=0), touch, 1, 1)
    chip_touch = jnp.minimum(counted[:chips], 1.0)
    block_touch = counted[chips:]
    any_touch = jnp.broadcast_to(jnp.max(block_touch, axis=0, keepdims=True), (8, reqs))
    of_group = lax.shift_right_logical(iota((reqs, reqs), 0), 2)
    before = ones_where(
        (of_group == lax.shift_right_logical(iota((reqs, reqs), 1), 2)) & (iota((reqs, reqs), 0) < iota((reqs, reqs), 1))
    )
    rank = dot(jnp.concatenate([chip_touch, any_touch], axis=0).astype(BF), before)
    rank, place = rank[:chips], rank[chips:]
    mine = ones_where(iota((reqs, 32), 0) == group * 4 + lax.shift_right_logical(iota((reqs, 32), 1), 3))
    core = lax.shift_right_logical(me, 4) & 1
    served = (core ^ (lax.shift_right_logical(iota((8, reqs), 1), 2) & 1)) + offset
    in_group = ones_where(lax.shift_right_logical(iota((reqs, 128), 0), 2) == iota((reqs, 128), 1))
    bits = jnp.where(place == served.astype(F32), block_touch, 0.0)
    sums = dot(jnp.concatenate([chip_touch, bits], axis=0).astype(BF), in_group)
    bits = sums[chips:]
    most = jnp.max(jnp.max(sums[:chips], axis=0, keepdims=True), axis=1, keepdims=True)
    table_ref[...] = jnp.where(iota((8, 128), 0) == 7, most, bits).astype(jnp.int32)
    first = ((group & 1) + offset).astype(F32)
    second = ((1 - (group & 1)) + offset).astype(F32)
    by_core = [jnp.where(rank == want, chip_touch, 0.0) for want in (first, second)]
    by_dev = [by_core[k][z * 16 : z * 16 + 16] for z in range(4) for k in (0, 1)]
    by_dev = dot(jnp.concatenate(by_dev, axis=0).astype(BF), mine)
    chosen = jnp.broadcast_to(by_dev[:, None, :], (DEVS, ROWS, 32)).reshape(n, 32)
    in_row = (iota((n, 32), 1) & 7) // SIDE == (iota((n, 32), 0) & (ROWS - 1))
    chosen = jnp.where(in_row, chosen, 0.0)
    route_ref[...] = chosen.astype(BF)
    by_place, spread = [], []
    q = q_ref[...].astype(F32)
    for j in range(SIDE):
        by_place.append(jnp.where((iota((n, 32), 1) & (SIDE - 1)) == j, chosen, 0.0))
        pieces = [jnp.zeros((32, j * LAT), F32), q[:, :LAT], jnp.zeros((32, (SIDE - 1 - j) * LAT), F32)]
        pieces += [jnp.zeros((32, j * (DK - LAT)), F32), q[:, LAT:], jnp.zeros((32, (SIDE - 1 - j) * (DK - LAT)), F32)]
        spread.append(jnp.concatenate([piece for piece in pieces if piece.shape[1]], axis=1))
    by_place = jnp.concatenate(by_place, axis=1).astype(BF)
    spread = jnp.concatenate(spread, axis=0).astype(BF)
    send_ref[...] = dot(by_place, spread).astype(BF).reshape(send_ref.shape)


def route(offset, me, q_rows, touch_mask, block_slot):
    n = DEVS * ROWS
    vmem = pl.BlockSpec(memory_space=pltpu.VMEM)
    return pl.pallas_call(
        functools.partial(route_kernel, offset),
        out_shape=(
            jax.ShapeDtypeStruct((DEVS, ROWS, SEND), BF),
            jax.ShapeDtypeStruct((n, 32), BF),
            jax.ShapeDtypeStruct((8, 128), jnp.int32),
        ),
        in_specs=[pl.BlockSpec(memory_space=pltpu.SMEM), vmem, vmem, vmem],
        out_specs=(vmem, vmem, vmem),
        compiler_params=pltpu.CompilerParams(vmem_limit_bytes=32 * MIB),
        cost_estimate=pl.CostEstimate(flops=2 * n * 32 * 1024, bytes_accessed=2 * n * SEND, transcendentals=0),
        name="route",
    )(me, q_rows, touch_mask, block_slot.reshape(1, -1))


LOG2_E = 1.4426950408889634
LN_2 = 0.6931471805599453


def holder_kernel(table_ref, packets_ref, own_ref, far_ref, out_ref, peer_ref, q, top, total, acc, out, todo, out_sems, peer_sem):
    fetch = pltpu.make_async_copy(far_ref, peer_ref, peer_sem)
    fetch.start()
    share = 16 * ROWS
    for g in range(GROUPS):
        x = packets_ref[g * 16 : g * 16 + 16].reshape(share, SEND)
        for j in range(SIDE):
            here = slice(j * share, j * share + share)
            q[g, here, :LAT] = x[:, j * LAT : j * LAT + LAT]
            rotary = SIDE * LAT + j * (DK - LAT)
            q[g, here, LAT:] = x[:, rotary : rotary + DK - LAT]
    counts = []
    for b in range(4):
        count = jnp.int32(0)
        for g in range(GROUPS):
            todo[b, count] = g
            count = count + jnp.where(table_ref[b, g] > 0, 1, 0)
        todo[b, count] = GROUPS
        counts.append(count)
    top[...] = jnp.full(top.shape, MASKED_SCORE, F32)
    total[...] = jnp.ones(total.shape, F32)
    acc[...] = jnp.zeros(acc.shape, F32)
    def work(ref, units):
        c = SOFTMAX_SCALE * LOG2_E
        scores = []
        for block, pair in units:
            rows = jnp.concatenate([q[jnp.minimum(g, GROUPS - 1)] for g in pair], axis=0)
            scores.append(dot(rows[:, :LAT], ref[block, :LAT, :]) + dot(rows[:, LAT:], ref[block, LAT:, :]))
        for s, (block, pair) in zip(scores, units):
            old = jnp.concatenate([top[g] for g in pair], axis=0)
            new = jnp.maximum(old, jnp.max(s, axis=1, keepdims=True) * c)
            scale = jnp.exp2(old - new)
            p = jnp.exp2(s * c - new)
            added = jnp.sum(p, axis=1, keepdims=True)
            value = dot(p.astype(BF), ref[block, :LAT, :], 1, 1)
            for k, g in enumerate(pair):
                here = slice(k * GROUP_ROWS, (k + 1) * GROUP_ROWS)
                top[g] = new[here]
                total[g] = total[g] * scale[here] + added[here]
                acc[g] = acc[g] * scale[here] + value[here]

    for half, ref in enumerate((own_ref, peer_ref)):
        if half == 1:
            fetch.wait()
        pairs = [lax.shift_right_logical(counts[2 * half + k] + 1, 1) for k in (0, 1)]
        n = pairs[0] + pairs[1]

        def unit(u, half=half, pairs=pairs):
            block = jnp.where(u < pairs[0], 0, 1)
            i = 2 * (u - block * pairs[0])
            return block, [todo[2 * half + block, i], todo[2 * half + block, i + 1]]

        def step(i, carry, ref=ref, unit=unit):
            work(ref, [unit(2 * i), unit(2 * i + 1)])
            return carry

        lax.fori_loop(0, lax.shift_right_logical(n, 1), step, 0)

        @pl.when((n & 1) == 1)
        def _(ref=ref, unit=unit, n=n):
            work(ref, [unit(n - 1)])

    copies = []
    for g in range(GROUPS):
        value = acc[g] * (1.0 / total[g])
        lse = (top[g] + jnp.log2(total[g])) * LN_2
        high = lse.astype(BF).astype(F32)
        middle = (lse - high).astype(BF).astype(F32)
        low = lse - high - middle
        lane = iota((share, 128), 1)
        tail = jnp.where(lane == 3 * SIDE, 1.0, 0.0)
        for j in range(SIDE):
            for k, piece in enumerate((high, middle, low)):
                tail = jnp.where(lane == 3 * j + k, piece[j * share : j * share + share], tail)
        row = [value[j * share : j * share + share] for j in range(SIDE)] + [tail]
        row = jnp.concatenate(row, axis=1).astype(BF)
        here = pl.ds(g * 16, 16)
        out[here] = row.reshape(16, ROWS, PACK)
        copies.append(pltpu.make_async_copy(out.at[here], out_ref.at[here], out_sems.at[g]))
        copies[-1].start()
    for copy in copies:
        copy.wait()


def holder(table, queries, own, peer):
    vmem = pl.BlockSpec(memory_space=pltpu.VMEM)
    return pl.pallas_call(
        holder_kernel,
        out_shape=jax.ShapeDtypeStruct((DEVS, ROWS, PACK), BF),
        in_specs=[pl.BlockSpec(memory_space=pltpu.SMEM), vmem, vmem, pl.BlockSpec(memory_space=pl.ANY)],
        out_specs=pl.BlockSpec(memory_space=pl.ANY),
        scratch_shapes=[
            pltpu.VMEM((BLK_DEV, DK, BLK), BF),
            pltpu.VMEM((GROUPS, GROUP_ROWS, DK), BF),
            pltpu.VMEM((GROUPS + 1, GROUP_ROWS, 1), F32),
            pltpu.VMEM((GROUPS + 1, GROUP_ROWS, 1), F32),
            pltpu.VMEM((GROUPS + 1, GROUP_ROWS, LAT), F32),
            pltpu.VMEM((DEVS, ROWS, PACK), BF),
            pltpu.SMEM((4, 16), jnp.int32),
            pltpu.SemaphoreType.DMA((GROUPS,)),
            pltpu.SemaphoreType.DMA,
        ],
        compiler_params=pltpu.CompilerParams(vmem_limit_bytes=32 * MIB),
        cost_estimate=pl.CostEstimate(
            flops=2 * 1024 * 1024 * (DK + LAT), bytes_accessed=4 * 2 * BLK * DK, transcendentals=1024 * 1024
        ),
        name="holder",
    )(table, queries, own, peer)


def suffix_kernel(len_ref, q_ref, kv_ref, out_ref, lse_ref):
    r = pl.program_id(0)
    kv = kv_ref[0]
    s = dot(q_ref[0], kv) * SOFTMAX_SCALE
    s = jnp.where(iota(s.shape, 1) < len_ref[r], s, MASKED_SCORE)
    top = jnp.max(s, axis=1, keepdims=True)
    p = jnp.exp(s - top)
    total = jnp.sum(p, axis=1, keepdims=True)
    out_ref[0] = dot(p.astype(BF), kv[:LAT], 1, 1) / total
    lse_ref[0] = jnp.broadcast_to(top + jnp.log(total), lse_ref.shape[1:])


def suffix(lengths, queries, cache):
    reqs, heads, _ = queries.shape
    return pl.pallas_call(
        suffix_kernel,
        grid=(reqs,),
        out_shape=(
            jax.ShapeDtypeStruct((reqs, heads, LAT), F32),
            jax.ShapeDtypeStruct((reqs, heads, 128), F32),
        ),
        in_specs=[
            pl.BlockSpec(memory_space=pltpu.SMEM),
            pl.BlockSpec((1, heads, DK), lambda r: (r, 0, 0)),
            pl.BlockSpec((1, DK, SUF), lambda r: (r, 0, 0)),
        ],
        out_specs=(
            pl.BlockSpec((1, heads, LAT), lambda r: (r, 0, 0)),
            pl.BlockSpec((1, heads, 128), lambda r: (r, 0, 0)),
        ),
        compiler_params=pltpu.CompilerParams(vmem_limit_bytes=32 * MIB),
        cost_estimate=pl.CostEstimate(
            flops=2 * 4 * 256 * 1024 * (DK + LAT), bytes_accessed=4 * 2 * SUF * DK, transcendentals=4 * 8 * 1024
        ),
        name="suffix",
    )(lengths, queries, cache)


def merge_kernel(rounds, *refs):
    parts, routes = refs[:rounds], refs[rounds : 2 * rounds]
    suffix_ref, suffix_lse_ref, out_ref, lse_ref = refs[2 * rounds :]
    heads = 32
    eye = iota((heads, heads), 0) == iota((heads, heads), 1)
    suffix_lse = suffix_lse_ref[:, :1]
    ceiling = jnp.max(jnp.where(eye, suffix_lse, MASKED_SCORE), axis=0, keepdims=True)
    scores = []
    n = DEVS * ROWS
    flat = [part[...].reshape(n, PACK) for part in parts]
    place = iota((n, heads), 1) & (SIDE - 1)
    for part, chosen in zip(flat, routes):
        tail = part[:, SIDE * LAT :].astype(F32)
        score = MASKED_SCORE
        for j in range(SIDE):
            lse = tail[:, 3 * j : 3 * j + 1] + tail[:, 3 * j + 1 : 3 * j + 2] + tail[:, 3 * j + 2 : 3 * j + 3]
            score = jnp.where(place == j, lse, score)
        score = jnp.where(chosen[...] > 0.5, score, MASKED_SCORE)
        scores.append(score)
        ceiling = jnp.maximum(ceiling, jnp.max(score, axis=0, keepdims=True))
    top = jnp.max(jnp.where(eye, ceiling, MASKED_SCORE), axis=1, keepdims=True)
    weight = jnp.exp(suffix_lse - top)
    merged = weight * suffix_ref[...]
    total = weight
    place = iota((heads, LAT), 0) & (SIDE - 1)
    for part, score in zip(flat, scores):
        w = jnp.exp(score - ceiling)
        high = w.astype(BF)
        low = (w - high.astype(F32)).astype(BF)
        both = jnp.concatenate([high, low], axis=1).T
        sums = dot(both, part)
        sums = sums[:heads] + sums[heads:]
        total = total + sums[:, SIDE * LAT + 3 * SIDE : SIDE * LAT + 3 * SIDE + 1]
        for j in range(SIDE):
            merged = merged + jnp.where(place == j, sums[:, j * LAT : j * LAT + LAT], 0.0)
    out = (merged / total).astype(BF)
    lse = top + jnp.log(total)
    diagonal = iota((8, 8), 0) == iota((8, 8), 1)
    for q in range(4):
        out_ref[q] = out[q * 8 : q * 8 + 8]
        column = jnp.where(diagonal, lse[q * 8 : q * 8 + 8], 0.0)
        lse_ref[q : q + 1, :] = jnp.sum(column, axis=0, keepdims=True)


def merge(parts, routes, suffix_out, suffix_lse):
    vmem = pl.BlockSpec(memory_space=pltpu.VMEM)
    return pl.pallas_call(
        functools.partial(merge_kernel, len(parts)),
        out_shape=(jax.ShapeDtypeStruct((4, 8, LAT), BF), jax.ShapeDtypeStruct((4, 8), F32)),
        in_specs=[vmem] * (2 * len(parts) + 2),
        out_specs=(vmem, vmem),
        compiler_params=pltpu.CompilerParams(vmem_limit_bytes=32 * MIB),
        name="merge",
    )(*parts, *routes, suffix_out, suffix_lse)


AXES = ("z", "core", "x", "y")


def on_device(queries, prefix_cache, suffix_cache, suffix_len, touch_mask, block_slot):
    reqs, heads, _ = queries.shape
    me = lax.axis_index(AXES).astype(jnp.int32).reshape(1)
    q_rows = queries.reshape(reqs * heads, DK)
    own = prefix_cache.transpose(0, 2, 1)
    peer = lax.ppermute(own, "core", [(0, 1), (1, 0)])

    def one_round(offset, peer):
        send, chosen, table = route(offset, me, q_rows, touch_mask, block_slot)
        got = lax.all_to_all(send, AXES, split_axis=0, concat_axis=0, tiled=True)
        parts = holder(table, got, own, peer)
        parts = lax.all_to_all(parts, AXES, split_axis=0, concat_axis=0, tiled=True)
        return parts, chosen, table

    parts, chosen, table = one_round(0, peer)
    suffix_out, suffix_lse = suffix(suffix_len, queries, suffix_cache.transpose(0, 2, 1))
    suffix_out = suffix_out.reshape(reqs * heads, LAT)
    suffix_lse = suffix_lse.reshape(reqs * heads, 128)

    def one(parts, chosen, peer):
        return merge([parts], [chosen], suffix_out, suffix_lse)

    def two(parts, chosen, peer):
        more, more_chosen, _ = one_round(2, peer)
        return merge([parts, more], [chosen, more_chosen], suffix_out, suffix_lse)

    return tuple(lax.cond(table[7, 0] > 2, two, one, parts, chosen, peer))


def solution(mesh):
    grid = Mesh(mesh.devices.reshape(4, 2, 4, 4), AXES)
    rows, cache = ("z", "core"), ("x", "y")
    in_specs = (
        P(rows, cache, None),
        P(AXES, None, None),
        P(rows, None, None),
        P(rows),
        P(),
        P(),
    )
    out_specs = (P(rows, cache, None), P(rows, cache))
    return jax.shard_map(
        on_device, mesh=grid, in_specs=in_specs, out_specs=out_specs, check_vma=False
    )
```

```python
import functools
import jax
import jax.numpy as jnp
from jax import lax
from jax.experimental import pallas as pl
from jax.experimental.pallas import tpu as pltpu
from jax.sharding import Mesh, PartitionSpec as P

H = 128
LAT = 512
DK = 576
BLK = 1024
BLK_DEV = 2
SUF = 1024
DEVS = 128
SIDE = 2
ROWS = 8 // SIDE
SEND = SIDE * DK
PACK = SIDE * LAT + 128
GROUPS = 8
GROUP_ROWS = 128

SOFTMAX_SCALE = 192.0 ** (-0.5)
MASKED_SCORE = -1e30
BF = jnp.bfloat16
F32 = jnp.float32
MIB = 1024 * 1024


def iota(shape, dim):
    return lax.broadcasted_iota(jnp.int32, shape, dim)


def ones_where(mask):
    return jnp.where(mask, 1.0, 0.0).astype(BF)


def dot(a, b, ca=1, cb=0):
    return lax.dot_general(a, b, (((ca,), (cb,)), ((), ())), preferred_element_type=F32)


def route_kernel(offset, me_ref, q_ref, touch_ref, slot_ref, send_ref, route_ref, table_ref):
    me = me_ref[0]
    group = lax.shift_right_logical(me, 4)
    n = DEVS * ROWS
    chips = DEVS // 2
    touch = touch_ref[...].astype(F32).astype(BF)
    reqs, blocks = touch.shape
    slots = slot_ref[...]
    chip_of = lax.shift_right_logical(slots, 6) * 16 + (lax.shift_right_logical(slots, 1) & 15)
    b = iota((8, blocks), 0)
    wanted = jnp.where(b < 4, jnp.where(b < 2, me, me ^ 16) * 2 + (b & 1), -1)
    rows = [ones_where(iota((chips, blocks), 0) == chip_of), ones_where(slots == wanted)]
    counted = dot(jnp.concatenate(rows, axis=0), touch, 1, 1)
    chip_touch = jnp.minimum(counted[:chips], 1.0)
    block_touch = counted[chips:]
    any_touch = jnp.broadcast_to(jnp.max(block_touch, axis=0, keepdims=True), (8, reqs))
    of_group = lax.shift_right_logical(iota((reqs, reqs), 0), 2)
    before = ones_where(
        (of_group == lax.shift_right_logical(iota((reqs, reqs), 1), 2)) & (iota((reqs, reqs), 0) < iota((reqs, reqs), 1))
    )
    rank = dot(jnp.concatenate([chip_touch, any_touch], axis=0).astype(BF), before)
    rank, place = rank[:chips], rank[chips:]
    mine = ones_where(iota((reqs, 32), 0) == group * 4 + lax.shift_right_logical(iota((reqs, 32), 1), 3))
    core = lax.shift_right_logical(me, 4) & 1
    served = (core ^ (lax.shift_right_logical(iota((8, reqs), 1), 2) & 1)) + offset
    in_group = ones_where(lax.shift_right_logical(iota((reqs, 128), 0), 2) == iota((reqs, 128), 1))
    bits = jnp.where(place == served.astype(F32), block_touch, 0.0)
    sums = dot(jnp.concatenate([chip_touch, bits], axis=0).astype(BF), in_group)
    bits = sums[chips:]
    most = jnp.max(jnp.max(sums[:chips], axis=0, keepdims=True), axis=1, keepdims=True)
    table_ref[...] = jnp.where(iota((8, 128), 0) == 7, most, bits).astype(jnp.int32)
    first = ((group & 1) + offset).astype(F32)
    second = ((1 - (group & 1)) + offset).astype(F32)
    by_core = [jnp.where(rank == want, chip_touch, 0.0) for want in (first, second)]
    by_dev = [by_core[k][z * 16 : z * 16 + 16] for z in range(4) for k in (0, 1)]
    by_dev = dot(jnp.concatenate(by_dev, axis=0).astype(BF), mine)
    chosen = jnp.broadcast_to(by_dev[:, None, :], (DEVS, ROWS, 32)).reshape(n, 32)
    in_row = (iota((n, 32), 1) & 7) // SIDE == (iota((n, 32), 0) & (ROWS - 1))
    chosen = jnp.where(in_row, chosen, 0.0)
    route_ref[...] = chosen.astype(BF)
    by_place, spread = [], []
    q = q_ref[...].astype(F32)
    for j in range(SIDE):
        by_place.append(jnp.where((iota((n, 32), 1) & (SIDE - 1)) == j, chosen, 0.0))
        pieces = [jnp.zeros((32, j * LAT), F32), q[:, :LAT], jnp.zeros((32, (SIDE - 1 - j) * LAT), F32)]
        pieces += [jnp.zeros((32, j * (DK - LAT)), F32), q[:, LAT:], jnp.zeros((32, (SIDE - 1 - j) * (DK - LAT)), F32)]
        spread.append(jnp.concatenate([piece for piece in pieces if piece.shape[1]], axis=1))
    by_place = jnp.concatenate(by_place, axis=1).astype(BF)
    spread = jnp.concatenate(spread, axis=0).astype(BF)
    send_ref[...] = dot(by_place, spread).astype(BF).reshape(send_ref.shape)


def route(offset, me, q_rows, touch_mask, block_slot):
    n = DEVS * ROWS
    vmem = pl.BlockSpec(memory_space=pltpu.VMEM)
    return pl.pallas_call(
        functools.partial(route_kernel, offset),
        out_shape=(
            jax.ShapeDtypeStruct((DEVS, ROWS, SEND), BF),
            jax.ShapeDtypeStruct((n, 32), BF),
            jax.ShapeDtypeStruct((8, 128), jnp.int32),
        ),
        in_specs=[pl.BlockSpec(memory_space=pltpu.SMEM), vmem, vmem, vmem],
        out_specs=(vmem, vmem, vmem),
        compiler_params=pltpu.CompilerParams(vmem_limit_bytes=32 * MIB),
        cost_estimate=pl.CostEstimate(flops=2 * n * 32 * 1024, bytes_accessed=2 * n * SEND, transcendentals=0),
        name="route",
    )(me, q_rows, touch_mask, block_slot.reshape(1, -1))


LOG2_E = 1.4426950408889634
LN_2 = 0.6931471805599453


def holder_kernel(table_ref, packets_ref, own_ref, far_ref, out_ref, peer_ref, q, top, total, acc, out, todo, out_sems, peer_sem):
    fetch = pltpu.make_async_copy(far_ref, peer_ref, peer_sem)
    fetch.start()
    share = 16 * ROWS
    for g in range(GROUPS):
        x = packets_ref[g * 16 : g * 16 + 16].reshape(share, SEND)
        for j in range(SIDE):
            here = slice(j * share, j * share + share)
            q[g, here, :LAT] = x[:, j * LAT : j * LAT + LAT]
            rotary = SIDE * LAT + j * (DK - LAT)
            q[g, here, LAT:] = x[:, rotary : rotary + DK - LAT]
    counts = []
    for b in range(4):
        count = jnp.int32(0)
        for g in range(GROUPS):
            todo[b, count] = g
            count = count + jnp.where(table_ref[b, g] > 0, 1, 0)
        todo[b, count] = GROUPS
        counts.append(count)
    top[...] = jnp.full(top.shape, MASKED_SCORE, F32)
    total[...] = jnp.ones(total.shape, F32)
    acc[...] = jnp.zeros(acc.shape, F32)
    def work(ref, units):
        c = SOFTMAX_SCALE * LOG2_E
        scores = []
        for block, pair in units:
            rows = jnp.concatenate([q[jnp.minimum(g, GROUPS - 1)] for g in pair], axis=0)
            scores.append(dot(rows[:, :LAT], ref[block, :LAT, :]) + dot(rows[:, LAT:], ref[block, LAT:, :]))
        for s, (block, pair) in zip(scores, units):
            old = jnp.concatenate([top[g] for g in pair], axis=0)
            new = jnp.maximum(old, jnp.max(s, axis=1, keepdims=True) * c)
            scale = jnp.exp2(old - new)
            p = jnp.exp2(s * c - new)
            added = jnp.sum(p, axis=1, keepdims=True)
            value = dot(p.astype(BF), ref[block, :LAT, :], 1, 1)
            for k, g in enumerate(pair):
                here = slice(k * GROUP_ROWS, (k + 1) * GROUP_ROWS)
                top[g] = new[here]
                total[g] = total[g] * scale[here] + added[here]
                acc[g] = acc[g] * scale[here] + value[here]

    for half, ref in enumerate((own_ref, peer_ref)):
        if half == 1:
            fetch.wait()
        many = [jnp.where(counts[2 * half + k] >= 7, 1, 0) for k in (0, 1)]

        def wide(block, carry, half=half, ref=ref, many=many):
            @pl.when(jnp.where(block == 0, many[0], many[1]) == 1)
            def _():
                work(ref, [(block, [todo[2 * half + block, 4 * j + k] for k in range(4)]) for j in (0, 1)])

            return carry

        lax.fori_loop(0, 2, wide, 0)
        pairs = [lax.shift_right_logical(counts[2 * half + k] + 1, 1) * (1 - many[k]) for k in (0, 1)]
        n = pairs[0] + pairs[1]

        def unit(u, half=half, pairs=pairs):
            block = jnp.where(u < pairs[0], 0, 1)
            i = 2 * (u - block * pairs[0])
            return block, [todo[2 * half + block, i], todo[2 * half + block, i + 1]]

        def step(i, carry, ref=ref, unit=unit):
            work(ref, [unit(2 * i), unit(2 * i + 1)])
            return carry

        lax.fori_loop(0, lax.shift_right_logical(n, 1), step, 0)

        @pl.when((n & 1) == 1)
        def _(ref=ref, unit=unit, n=n):
            work(ref, [unit(n - 1)])

    copies = []
    for g in range(GROUPS):
        value = acc[g] * (1.0 / total[g])
        lse = (top[g] + jnp.log2(total[g])) * LN_2
        high = lse.astype(BF).astype(F32)
        middle = (lse - high).astype(BF).astype(F32)
        low = lse - high - middle
        lane = iota((share, 128), 1)
        tail = jnp.where(lane == 3 * SIDE, 1.0, 0.0)
        for j in range(SIDE):
            for k, piece in enumerate((high, middle, low)):
                tail = jnp.where(lane == 3 * j + k, piece[j * share : j * share + share], tail)
        row = [value[j * share : j * share + share] for j in range(SIDE)] + [tail]
        row = jnp.concatenate(row, axis=1).astype(BF)
        here = pl.ds(g * 16, 16)
        out[here] = row.reshape(16, ROWS, PACK)
        copies.append(pltpu.make_async_copy(out.at[here], out_ref.at[here], out_sems.at[g]))
        copies[-1].start()
    for copy in copies:
        copy.wait()


def holder(table, queries, own, peer):
    vmem = pl.BlockSpec(memory_space=pltpu.VMEM)
    return pl.pallas_call(
        holder_kernel,
        out_shape=jax.ShapeDtypeStruct((DEVS, ROWS, PACK), BF),
        in_specs=[pl.BlockSpec(memory_space=pltpu.SMEM), vmem, vmem, pl.BlockSpec(memory_space=pl.ANY)],
        out_specs=pl.BlockSpec(memory_space=pl.ANY),
        scratch_shapes=[
            pltpu.VMEM((BLK_DEV, DK, BLK), BF),
            pltpu.VMEM((GROUPS, GROUP_ROWS, DK), BF),
            pltpu.VMEM((GROUPS + 1, GROUP_ROWS, 1), F32),
            pltpu.VMEM((GROUPS + 1, GROUP_ROWS, 1), F32),
            pltpu.VMEM((GROUPS + 1, GROUP_ROWS, LAT), F32),
            pltpu.VMEM((DEVS, ROWS, PACK), BF),
            pltpu.SMEM((4, 16), jnp.int32),
            pltpu.SemaphoreType.DMA((GROUPS,)),
            pltpu.SemaphoreType.DMA,
        ],
        compiler_params=pltpu.CompilerParams(vmem_limit_bytes=32 * MIB),
        cost_estimate=pl.CostEstimate(
            flops=2 * 1024 * 1024 * (DK + LAT), bytes_accessed=4 * 2 * BLK * DK, transcendentals=1024 * 1024
        ),
        name="holder",
    )(table, queries, own, peer)


def suffix_kernel(len_ref, q_ref, kv_ref, out_ref, lse_ref):
    r = pl.program_id(0)
    kv = kv_ref[0]
    s = dot(q_ref[0], kv) * SOFTMAX_SCALE
    s = jnp.where(iota(s.shape, 1) < len_ref[r], s, MASKED_SCORE)
    top = jnp.max(s, axis=1, keepdims=True)
    p = jnp.exp(s - top)
    total = jnp.sum(p, axis=1, keepdims=True)
    out_ref[0] = dot(p.astype(BF), kv[:LAT], 1, 1) / total
    lse_ref[0] = jnp.broadcast_to(top + jnp.log(total), lse_ref.shape[1:])


def suffix(lengths, queries, cache):
    reqs, heads, _ = queries.shape
    return pl.pallas_call(
        suffix_kernel,
        grid=(reqs,),
        out_shape=(
            jax.ShapeDtypeStruct((reqs, heads, LAT), F32),
            jax.ShapeDtypeStruct((reqs, heads, 128), F32),
        ),
        in_specs=[
            pl.BlockSpec(memory_space=pltpu.SMEM),
            pl.BlockSpec((1, heads, DK), lambda r: (r, 0, 0)),
            pl.BlockSpec((1, DK, SUF), lambda r: (r, 0, 0)),
        ],
        out_specs=(
            pl.BlockSpec((1, heads, LAT), lambda r: (r, 0, 0)),
            pl.BlockSpec((1, heads, 128), lambda r: (r, 0, 0)),
        ),
        compiler_params=pltpu.CompilerParams(vmem_limit_bytes=32 * MIB),
        cost_estimate=pl.CostEstimate(
            flops=2 * 4 * 256 * 1024 * (DK + LAT), bytes_accessed=4 * 2 * SUF * DK, transcendentals=4 * 8 * 1024
        ),
        name="suffix",
    )(lengths, queries, cache)


def merge_kernel(rounds, *refs):
    parts, routes = refs[:rounds], refs[rounds : 2 * rounds]
    suffix_ref, suffix_lse_ref, out_ref, lse_ref = refs[2 * rounds :]
    heads = 32
    eye = iota((heads, heads), 0) == iota((heads, heads), 1)
    suffix_lse = suffix_lse_ref[:, :1]
    ceiling = jnp.max(jnp.where(eye, suffix_lse, MASKED_SCORE), axis=0, keepdims=True)
    scores = []
    n = DEVS * ROWS
    flat = [part[...].reshape(n, PACK) for part in parts]
    place = iota((n, heads), 1) & (SIDE - 1)
    for part, chosen in zip(flat, routes):
        tail = part[:, SIDE * LAT :].astype(F32)
        score = MASKED_SCORE
        for j in range(SIDE):
            lse = tail[:, 3 * j : 3 * j + 1] + tail[:, 3 * j + 1 : 3 * j + 2] + tail[:, 3 * j + 2 : 3 * j + 3]
            score = jnp.where(place == j, lse, score)
        score = jnp.where(chosen[...] > 0.5, score, MASKED_SCORE)
        scores.append(score)
        ceiling = jnp.maximum(ceiling, jnp.max(score, axis=0, keepdims=True))
    top = jnp.max(jnp.where(eye, ceiling, MASKED_SCORE), axis=1, keepdims=True)
    weight = jnp.exp(suffix_lse - top)
    merged = weight * suffix_ref[...]
    total = weight
    place = iota((heads, LAT), 0) & (SIDE - 1)
    for part, score in zip(flat, scores):
        w = jnp.exp(score - ceiling)
        high = w.astype(BF)
        low = (w - high.astype(F32)).astype(BF)
        both = jnp.concatenate([high, low], axis=1)
        sums = dot(both, part, 0, 0)
        sums = sums[:heads] + sums[heads:]
        total = total + sums[:, SIDE * LAT + 3 * SIDE : SIDE * LAT + 3 * SIDE + 1]
        for j in range(SIDE):
            merged = merged + jnp.where(place == j, sums[:, j * LAT : j * LAT + LAT], 0.0)
    out = (merged / total).astype(BF)
    lse = top + jnp.log(total)
    diagonal = iota((8, 8), 0) == iota((8, 8), 1)
    for q in range(4):
        out_ref[q] = out[q * 8 : q * 8 + 8]
        column = jnp.where(diagonal, lse[q * 8 : q * 8 + 8], 0.0)
        lse_ref[q : q + 1, :] = jnp.sum(column, axis=0, keepdims=True)


def merge(parts, routes, suffix_out, suffix_lse):
    vmem = pl.BlockSpec(memory_space=pltpu.VMEM)
    return pl.pallas_call(
        functools.partial(merge_kernel, len(parts)),
        out_shape=(jax.ShapeDtypeStruct((4, 8, LAT), BF), jax.ShapeDtypeStruct((4, 8), F32)),
        in_specs=[vmem] * (2 * len(parts) + 2),
        out_specs=(vmem, vmem),
        compiler_params=pltpu.CompilerParams(vmem_limit_bytes=32 * MIB),
        name="merge",
    )(*parts, *routes, suffix_out, suffix_lse)


AXES = ("z", "core", "x", "y")


def on_device(queries, prefix_cache, suffix_cache, suffix_len, touch_mask, block_slot):
    reqs, heads, _ = queries.shape
    me = lax.axis_index(AXES).astype(jnp.int32).reshape(1)
    q_rows = queries.reshape(reqs * heads, DK)
    own = prefix_cache.transpose(0, 2, 1)
    peer = lax.ppermute(own, "core", [(0, 1), (1, 0)])

    def one_round(offset, peer):
        send, chosen, table = route(offset, me, q_rows, touch_mask, block_slot)
        got = lax.all_to_all(send, AXES, split_axis=0, concat_axis=0, tiled=True)
        parts = holder(table, got, own, peer)
        parts = lax.all_to_all(parts, AXES, split_axis=0, concat_axis=0, tiled=True)
        return parts, chosen, table

    parts, chosen, table = one_round(0, peer)
    suffix_out, suffix_lse = suffix(suffix_len, queries, suffix_cache.transpose(0, 2, 1))
    suffix_out = suffix_out.reshape(reqs * heads, LAT)
    suffix_lse = suffix_lse.reshape(reqs * heads, 128)

    def one(parts, chosen, peer):
        return merge([parts], [chosen], suffix_out, suffix_lse)

    def two(parts, chosen, peer):
        more, more_chosen, _ = one_round(2, peer)
        return merge([parts, more], [chosen, more_chosen], suffix_out, suffix_lse)

    return tuple(lax.cond(table[7, 0] > 2, two, one, parts, chosen, peer))


def solution(mesh):
    grid = Mesh(mesh.devices.reshape(4, 2, 4, 4), AXES)
    rows, cache = ("z", "core"), ("x", "y")
    in_specs = (
        P(rows, cache, None),
        P(AXES, None, None),
        P(rows, None, None),
        P(rows),
        P(),
        P(),
    )
    out_specs = (P(rows, cache, None), P(rows, cache))
    return jax.shard_map(
        on_device, mesh=grid, in_specs=in_specs, out_specs=out_specs, check_vma=False
    )
```
